128 devices in a mesh: seq: 16 (over x, z), head: 8 (over y, core).
Axes of the slice: x: 4, y: 4, z: 4, core: 2. Of those that a mesh axis runs over, the one named last changes fastest.
Arguments:
- query: bfloat16 [4096, 73728], P('seq', 'head'), may hold values from -390 to 390
- latent_blocks: bfloat16 [2048, 36864], P('seq'), may hold values from -6 to 6
- index_keys: bfloat16 [2048, 8192], P('seq'), may hold values from -6 to 6
- index_query: bfloat16 [4096, 8192], P(('seq', 'head')), may hold values from -14 to 14
- index_weight: float32 [4096, 64], P(('seq', 'head')), may hold values from 0.1 to 1
- block_list: int32 [32, 32], P('seq'), may hold values from 0 to 2047, as said below
- list_len: int32 [32], P('seq'), may hold values from 8 to 32
- group_start: int32 [32], P('seq'), may hold values from 384 to 130944, as said below
Outputs:
- context: bfloat16 [4096, 65536], P('seq', 'head')
- row_loss: float32 [4096], P(('seq', 'head'))
- index_grad: float32 [4096, 8192], P(('seq', 'head'))
The draws below stay inside these ranges and needn't reach their ends.
Inputs may be any that keep to these rules, and one draw needn't show every extreme that they name: Group c belongs to the queries of seq index c // 2: its rows lie in blocks of that index's range of 128 blocks. group_start is a multiple of 64. `block_list`: the first list_len[c] entries of row c are distinct blocks that end no later than the group; entries past list_len[c] are padding. Exactly 8 used entries lie in the group's own seq index's range, the group's last block among them; at most 8 used entries of one row lie in any one index's range, so the lists of one index's 2 groups name at most 16 blocks (repeats counted) of any one index's range.
All inputs are finite; a program needn't handle non-finite values.
Results may differ from the reference program's by a relative error of at most 0.0046.
Values may be sent and summed in bfloat16 or wider, within the bound.
No kernel may reach another device: no remote copies, remote signals or barrier semaphores. Data moves between devices by JAX's collectives and lax.ppermute only.
A program may use at most 256 MiB of HBM per device.

```python
import math
import jax
import jax.numpy as jnp
from jax import lax

H = 128
LAT = 512
IH = 64
ID = 128
BLK = 64
NSEL = 32
GROUP = 128
CAPC = 8
CH_DEV = 2
BLK_DEV = 128
QK = 576
GROUPS = 32
ROWS = 4096
NBLK = 2048


def layout(key):
    key = jax.random.fold_in(key, 11)
    span = GROUP // BLK
    owners = NBLK // BLK_DEV
    device = jnp.arange(GROUPS, dtype=jnp.int32) // CH_DEV
    offset = jax.random.randint(jax.random.fold_in(key, 1), (GROUPS,), CAPC - span, BLK_DEV - span + 1)
    first = device * BLK_DEV + offset
    last = first + span - 1
    window = last[:, None] - (CAPC - 1) + jnp.arange(CAPC, dtype=jnp.int32)[None, :]
    hot = jax.random.randint(jax.random.fold_in(key, 2), (GROUPS,), 0, jnp.maximum(device, 1))
    perm_keys = jax.random.split(jax.random.fold_in(key, 3), GROUPS * owners)
    within = jax.vmap(lambda one_key: jax.random.permutation(one_key, BLK_DEV))(perm_keys)
    within = within.reshape(GROUPS, owners, BLK_DEV).astype(jnp.int32)
    owner_keys = jax.random.split(jax.random.fold_in(key, 4), GROUPS)
    order = jax.vmap(lambda one_key: jax.random.permutation(one_key, owners))(owner_keys).astype(jnp.int32)
    usable = (order < device[:, None]) & (order != hot[:, None])
    ranking = jnp.where(usable, 0, 1) * owners + jnp.arange(owners, dtype=jnp.int32)[None, :]
    others = jnp.take_along_axis(order, jnp.argsort(ranking, axis=1), 1)
    spare = NSEL - 2 * CAPC
    count_other = jnp.maximum(device - 1, 0)
    divisor = jnp.maximum(count_other, 1)
    step = jnp.arange(spare, dtype=jnp.int32)
    other_owner = jnp.take_along_axis(others, step[None, :] % divisor[:, None], 1)
    other_rank = jnp.minimum(step[None, :] // divisor[:, None], BLK_DEV - 1)
    group_idx = jnp.arange(GROUPS, dtype=jnp.int32)[:, None]
    other_block = other_owner * BLK_DEV + within[group_idx, other_owner, other_rank]
    other_cap = jnp.minimum(spare, count_other * CAPC).astype(jnp.int32)
    drawn = jax.random.randint(jax.random.fold_in(key, 5), (GROUPS,), 0, other_cap + 1).astype(jnp.int32)
    other_count = jnp.where(device == owners - 1, other_cap, drawn)
    other_live = step[None, :] < other_count[:, None]
    hot_block = hot[:, None] * BLK_DEV + within[group_idx, hot[:, None], jnp.arange(CAPC, dtype=jnp.int32)[None, :]]
    hot_live = jnp.broadcast_to((device >= 1)[:, None], (GROUPS, CAPC))
    blocks = jnp.concatenate([window, hot_block, other_block], 1)
    live = jnp.concatenate([jnp.ones((GROUPS, CAPC), bool), hot_live, other_live], 1)
    blocks = jnp.where(live, blocks, last[:, None]).astype(jnp.int32)
    length = jnp.sum(live.astype(jnp.int32), 1)
    return (blocks, length, (first * BLK).astype(jnp.int32))


def base_latent(key):
    values = jax.random.normal(jax.random.fold_in(key, 21), (NBLK, BLK, QK), jnp.float32)
    return jnp.clip(values, -6.0, 6.0)


def base_index_keys(key):
    values = jax.random.normal(jax.random.fold_in(key, 22), (NBLK, BLK, ID), jnp.float32)
    return jnp.clip(values, -6.0, 6.0)


def draw_block_list(key, part):
    return layout(key)[0]


def draw_list_len(key, part):
    return layout(key)[1]


def draw_group_start(key, part):
    return layout(key)[2]


def draw_latent_blocks(key, part):
    values = base_latent(key)
    return values.reshape(NBLK, BLK * QK).astype(jnp.bfloat16)


def draw_index_keys(key, part):
    values = base_index_keys(key)
    return values.reshape(NBLK, BLK * ID).astype(jnp.bfloat16)


def draw_query(key, part):
    key = jax.random.fold_in(key, 31)
    values = jnp.clip(jax.random.normal(key, (ROWS, H, QK), jnp.float32), -6.0, 6.0)
    return values.reshape(ROWS, H * QK).astype(jnp.bfloat16)


def draw_index_query(key, part):
    key = jax.random.fold_in(key, 41)
    values = jnp.clip(1.5 * jax.random.normal(key, (ROWS, IH, ID), jnp.float32), -9.0, 9.0)
    return values.reshape(ROWS, IH * ID).astype(jnp.bfloat16)


def shard_levels(stream_key, shape, pieces, least, high):
    gain = 1.0
    for axis_at, parts in pieces:
        draws = jax.random.uniform(jax.random.fold_in(jax.random.fold_in(stream_key, 6), axis_at), (parts,), jnp.float32, least / len(pieces), high / len(pieces))
        gain = gain * jnp.repeat(jnp.exp(draws), shape[axis_at] // parts).reshape((-1,) + (1,) * (len(shape) - 1 - axis_at))
    return gain


def setup_inputs(seed: int = 0) -> dict:
    seeds = jax.random.split(jax.random.key(seed), 9)
    return {
        "query": draw_query(jax.random.fold_in(seeds[8], 71), 0),
        "latent_blocks": draw_latent_blocks(jax.random.fold_in(seeds[8], 71), 0),
        "index_keys": draw_index_keys(jax.random.fold_in(seeds[8], 71), 0),
        "index_query": draw_index_query(jax.random.fold_in(seeds[8], 71), 0),
        "index_weight": jnp.clip(jnp.exp(math.log(1.0) - 2.3025851 * jax.random.uniform(seeds[4], (ROWS, IH), jnp.float32) ** shard_levels(seeds[4], (ROWS, IH), ((0, 128),), -0.2, 0.2)), 0.1, 1.0),
        "block_list": draw_block_list(jax.random.fold_in(seeds[8], 71), 0),
        "list_len": draw_list_len(jax.random.fold_in(seeds[8], 71), 0),
        "group_start": draw_group_start(jax.random.fold_in(seeds[8], 71), 0),
    }


SOFTMAX_SCALE = 192.0 ** -0.5
INDEX_SCALE = 128.0 ** -0.5


def group_mask(blocks, length, start, first_row, rows):
    slot = jnp.arange(NSEL * BLK, dtype=jnp.int32) // BLK
    offset = jnp.arange(NSEL * BLK, dtype=jnp.int32) % BLK
    key_pos = jnp.take(blocks, slot).astype(jnp.int32) * BLK + offset
    query_pos = start + first_row + jnp.arange(rows, dtype=jnp.int32)
    return (slot < length)[None, :] & (key_pos[None, :] <= query_pos[:, None])


def attend(q_rows, keys, visible):
    rows = q_rows.shape[0]
    heads = q_rows.shape[1] // QK
    q_heads = q_rows.reshape(rows, heads, QK).astype(jnp.float32)
    scores = jnp.einsum("rhd,kd->hrk", q_heads, keys.astype(jnp.float32)) * SOFTMAX_SCALE
    scores = jnp.where(visible[None], scores, -jnp.inf)
    top = jnp.max(scores, -1, keepdims=True)
    weights = jnp.exp(scores - top)
    probs = weights / jnp.sum(weights, -1, keepdims=True)
    rounded = lax.optimization_barrier(probs.astype(jnp.bfloat16))
    context = jnp.einsum("hrk,kd->rhd", rounded.astype(jnp.float32), keys[:, :LAT].astype(jnp.float32))
    return context.astype(jnp.bfloat16).reshape(rows, heads * LAT), jnp.sum(probs, 0)


def indexer_rows(index_rows, weight_rows, key_sel, target, visible):
    rows = index_rows.shape[0]
    index_heads = index_rows.reshape(rows, IH, ID).astype(jnp.float32)
    activity = jnp.einsum("rjd,kd->rjk", index_heads, key_sel.astype(jnp.float32))
    logits = jnp.sum(jnp.maximum(activity, 0.0) * weight_rows[:, :, None], 1) * INDEX_SCALE
    logits = jnp.where(visible, logits, -jnp.inf)
    top = jnp.max(logits, -1, keepdims=True)
    shifted = logits - top
    log_q = shifted - jnp.log(jnp.sum(jnp.exp(shifted), -1, keepdims=True))
    prob_q = jnp.where(visible, jnp.exp(log_q), 0.0)
    live = visible & (target > 0)
    safe = jnp.where(live, target, 1.0)
    loss = jnp.sum(jnp.where(live, target * (jnp.log(safe) - log_q), 0.0), -1)
    diff = prob_q - target
    coef = jnp.where(activity > 0, diff[:, None, :] * weight_rows[:, :, None] * INDEX_SCALE, 0.0)
    coef = lax.optimization_barrier(coef.astype(jnp.bfloat16))
    grad = jnp.einsum("rjk,kd->rjd", coef.astype(jnp.float32), key_sel.astype(jnp.float32))
    return loss, grad.reshape(rows, IH * ID)


def reference(query, latent_blocks, index_keys, index_query, index_weight, block_list, list_len, group_start):
    def one(pack):
        rows, index_rows, weight_rows, blocks, length, start = pack
        keys = jnp.take(latent_blocks, blocks, axis=0).reshape(NSEL * BLK, QK)
        key_sel = jnp.take(index_keys, blocks, axis=0).reshape(NSEL * BLK, ID)
        visible = group_mask(blocks, length, start, 0, GROUP)
        context, partial_value = attend(rows, keys, visible)
        target = partial_value / H
        loss, grad = indexer_rows(index_rows, weight_rows, key_sel, target, visible)
        return context, loss, grad

    packs = (query.reshape(GROUPS, GROUP, H * QK), index_query.reshape(GROUPS, GROUP, IH * ID),
             index_weight.reshape(GROUPS, GROUP, IH), block_list, list_len, group_start)
    context, loss, grad = lax.map(one, packs)
    return context.reshape(ROWS, H * LAT), loss.reshape(ROWS), grad.reshape(ROWS, IH * ID)
```

```python
import functools
import math

import jax
import jax.numpy as jnp
from jax import lax
from jax.experimental import pallas as pl
from jax.experimental.pallas import tpu as pltpu
from jax.sharding import PartitionSpec as P

H = 128
LAT = 512
IH = 64
ID = 128
BLK = 64
NSEL = 32
GROUP = 128
CAPC = 8
QK = 576

PAIR = 2 * QK
KW = 640
SCALE = 192.0 ** -0.5
INDEX_SCALE = 128.0 ** -0.5
LOG2E = math.log2(math.e)
NEG = -1e30
OWN = CAPC * BLK
REM = NSEL - CAPC
VMEM_LIMIT = 56 * 1024 * 1024

f32 = jnp.float32
bf16 = jnp.bfloat16
i32 = jnp.int32


def params(n=1):
    return pltpu.CompilerParams(
        vmem_limit_bytes=VMEM_LIMIT, dimension_semantics=("arbitrary",) * n
    )


def smem():
    return pl.BlockSpec(memory_space=pltpu.SMEM)


def vmem():
    return pl.BlockSpec(memory_space=pltpu.VMEM)


def nt(a, b):
    return lax.dot_general(a, b, (((1,), (1,)), ((), ())), preferred_element_type=f32)


def nn(a, b):
    return jnp.dot(a, b, preferred_element_type=f32)


def plan_kernel(seqs, blk_dev, me_ref, list_ref, len_ref, req_ref, place_ref, own_ref, count):
    cap = 2 * CAPC
    me = me_ref[0]

    def clear_row(o, carry):
        count[o] = 0

        def clear(r, c):
            req_ref[o, r] = -1
            return c

        return lax.fori_loop(0, cap, clear, carry)

    lax.fori_loop(0, seqs, clear_row, 0)
    for g in range(2):

        def clear_place(r, c):
            place_ref[g * REM + r] = -1
            return c

        lax.fori_loop(0, REM, clear_place, 0)
        for r in range(CAPC):
            own_ref[g * CAPC + r] = -1

        def entry(k, carry):
            own_n, rem_n = carry
            block = list_ref[g, k]
            owner = block // blk_dev
            local = block - owner * blk_dev
            mine = owner == me

            @pl.when(mine)
            def _():
                own_ref[g * CAPC + jnp.minimum(own_n, CAPC - 1)] = local

            @pl.when(jnp.logical_not(mine))
            def _():
                rank = jnp.minimum(count[owner], cap - 1)
                count[owner] = rank + 1
                req_ref[owner, rank] = local
                place_ref[g * REM + jnp.minimum(rem_n, REM - 1)] = owner * cap + rank

            step = mine.astype(i32)
            return own_n + step, rem_n + 1 - step

        lax.fori_loop(0, len_ref[g], entry, (jnp.int32(0), jnp.int32(0)))


def plan(me, lists, lens, seqs, blk_dev):
    return pl.pallas_call(
        functools.partial(plan_kernel, seqs, blk_dev),
        out_shape=(
            jax.ShapeDtypeStruct((seqs, 2 * CAPC), i32),
            jax.ShapeDtypeStruct((2 * REM,), i32),
            jax.ShapeDtypeStruct((2 * CAPC,), i32),
        ),
        in_specs=[smem()] * 3,
        out_specs=(smem(),) * 3,
        scratch_shapes=[pltpu.SMEM((seqs,), i32)],
    )(me, lists, lens)


def send_kernel(h_ref, asked_ref, lat_ref, key_ref, lat_out, key_out):
    rows, blocks = asked_ref.shape[0], lat_ref.shape[0]
    lane = lax.broadcasted_iota(i32, (rows, blocks), 1)
    pick = (asked_ref[...] == lane).astype(f32).astype(bf16)
    lat_out[...] = nn(pick, lat_ref[...]).astype(bf16)
    key_out[...] = nn(pick, key_ref[...]).astype(bf16)


def send(h, asked, latent, keys, heads):
    rows = asked.shape[0]
    blocks = latent.shape[0]
    steps = 4
    lw = latent.shape[1] // heads // steps
    kw = keys.shape[1] // heads // steps
    return pl.pallas_call(
        send_kernel,
        out_shape=(
            jax.ShapeDtypeStruct((rows, lw * steps), bf16),
            jax.ShapeDtypeStruct((rows, kw * steps), bf16),
        ),
        grid_spec=pltpu.PrefetchScalarGridSpec(
            num_scalar_prefetch=1,
            grid=(steps,),
            in_specs=[
                pl.BlockSpec((rows, 1), lambda c, h: (0, 0)),
                pl.BlockSpec((blocks, lw), lambda c, h: (0, h[0] * steps + c)),
                pl.BlockSpec((blocks, kw), lambda c, h: (0, h[0] * steps + c)),
            ],
            out_specs=(
                pl.BlockSpec((rows, lw), lambda c, h: (0, c)),
                pl.BlockSpec((rows, kw), lambda c, h: (0, c)),
            ),
        ),
        compiler_params=params(),
    )(h, asked, latent, keys)


def picker(idx_ref, rows, width):
    row = lax.broadcasted_iota(i32, (rows, width), 0)
    lane = lax.broadcasted_iota(i32, (rows, width), 1)
    want = jnp.full((rows, width), -1, i32)
    for r in range(rows):
        want = jnp.where(row == r, idx_ref[r], want)
    return (want == lane).astype(f32).astype(bf16)


def own_kernel(idx_ref, lat_ref, key_ref, lat_out, key_out):
    pick = picker(idx_ref, 2 * CAPC, lat_ref.shape[0])
    pairs = lat_ref.shape[1] // PAIR
    got = [nn(pick, lat_ref[:, i * PAIR : (i + 1) * PAIR]) for i in range(pairs)]
    for g in range(2):
        part = [x[g * CAPC : (g + 1) * CAPC] for x in got]
        lat_out[g] = jnp.concatenate(part, 0).astype(bf16)
    got = [nn(pick, key_ref[:, t * ID : (t + 1) * ID]) for t in range(2 * pairs)]
    for g in range(2):
        for par in range(2):
            part = [x[g * CAPC : (g + 1) * CAPC] for x in got[par::2]]
            key_out[g, par] = jnp.concatenate(part, 0).astype(bf16)


def own_rows(idx, latent, keys):
    blocks = latent.shape[0]
    steps = 8
    pairs = BLK // 2 // steps
    rows = pairs * CAPC
    return pl.pallas_call(
        own_kernel,
        out_shape=(
            jax.ShapeDtypeStruct((2, OWN // 2, PAIR), bf16),
            jax.ShapeDtypeStruct((2, 2, OWN // 2, ID), bf16),
        ),
        grid=(steps,),
        in_specs=[
            smem(),
            pl.BlockSpec((blocks, pairs * PAIR), lambda c: (0, c)),
            pl.BlockSpec((blocks, 2 * pairs * ID), lambda c: (0, c)),
        ],
        out_specs=(
            pl.BlockSpec((2, rows, PAIR), lambda c: (0, c, 0)),
            pl.BlockSpec((2, 2, rows, ID), lambda c: (0, 0, c, 0)),
        ),
        compiler_params=params(),
    )(idx, latent, keys)


def pack_lat_kernel(idx_ref, lat_ref, lat_out):
    pick = picker(idx_ref, 2 * REM, lat_ref.shape[0])
    pairs = lat_ref.shape[1] // PAIR
    got = [nn(pick, lat_ref[:, i * PAIR : (i + 1) * PAIR]) for i in range(pairs)]
    for g in range(2):
        part = [x[g * REM : (g + 1) * REM] for x in got]
        lat_out[g] = jnp.concatenate(part, 0).astype(bf16)


def pack_lat(idx, lat):
    pairs = lat.shape[1] // PAIR
    return pl.pallas_call(
        pack_lat_kernel,
        out_shape=jax.ShapeDtypeStruct((2, pairs * REM, PAIR), bf16),
        in_specs=[smem(), vmem()],
        out_specs=vmem(),
        compiler_params=params(0),
    )(idx, lat)


def pack_key_kernel(idx_ref, key_ref, key_out):
    pick = picker(idx_ref, 2 * REM, key_ref.shape[0])
    heads = key_out.shape[0]
    tokens = key_ref.shape[1] // ID
    got = [nn(pick, key_ref[:, t * ID : (t + 1) * ID]) for t in range(tokens)]
    for g in range(2):
        part = [x[g * REM : (g + 1) * REM] for x in got[0::2] + got[1::2]]
        rows = jnp.concatenate(part, 0).astype(bf16)
        for d in range(heads // 2):
            key_out[g * (heads // 2) + d] = rows


def pack_key(idx, keys, heads):
    tokens = keys.shape[1] // ID
    return pl.pallas_call(
        pack_key_kernel,
        out_shape=jax.ShapeDtypeStruct((heads, tokens * REM, ID), bf16),
        in_specs=[smem(), vmem()],
        out_specs=vmem(),
        compiler_params=params(0),
    )(idx, keys)


def place_keys(x, ka, kb, at, rows):
    xf = x.astype(f32)
    lane = lax.broadcasted_iota(i32, (rows, KW), 1)
    gap = KW - QK
    even = jnp.where(lane < QK, xf[:, :KW], 0.0)
    odd = jnp.where(lane >= gap, xf[:, PAIR - KW :], 0.0)
    ka[pl.ds(at, rows), :] = even.astype(bf16)
    kb[pl.ds(at, rows), :] = pltpu.roll(even, gap, 1).astype(bf16)
    kb[pl.ds(at + rows, rows), :] = odd.astype(bf16)
    ka[pl.ds(at + rows, rows), :] = pltpu.roll(odd, QK, 1).astype(bf16)


def attend_kernel(src_ref, q_ref, own_ref, *refs):
    pieces, (bias_own, bias_rem, ctx_ref, t_ref, ka, kb, total) = refs[:8], refs[8:]
    step = pl.program_id(1)

    @pl.when(step == 0)
    def _():
        place_keys(own_ref[...], ka, kb, 0, own_ref.shape[0])
        for n, piece in enumerate(pieces):
            rows = piece.shape[0]
            at = pl.multiple_of(OWN + src_ref[n] * (2 * rows), 2 * rows)
            place_keys(piece[...], ka, kb, at, rows)
        total[...] = jnp.zeros_like(total)

    q = q_ref[...]
    pairs = q.shape[1] // PAIR
    own_b = jnp.concatenate([bias_own[...]] * pairs, 0)
    rem_b = bias_rem[...]
    for par, keys in ((0, ka), (1, kb)):
        first = [n * PAIR + par * (PAIR - KW) for n in range(pairs)]
        rows = jnp.concatenate([q[:, c : c + KW] for c in first], 0)
        s = nt(rows, keys[...])
        s_own = s[:, :OWN] + own_b
        s_rem = s[:, OWN:] + rem_b
        top = jnp.maximum(
            jnp.max(s_own, -1, keepdims=True), jnp.max(s_rem, -1, keepdims=True)
        )
        s = jnp.concatenate([s_own, s_rem], 1)
        w = jnp.exp2((s - top) * (SCALE * LOG2E))
        probs = w * (1.0 / jnp.sum(w, -1, keepdims=True))
        add = probs[:GROUP]
        for n in range(1, pairs):
            add = add + probs[n * GROUP : (n + 1) * GROUP]
        total[...] += add
        out = nn(probs.astype(bf16), ka[:, :LAT]).astype(bf16)
        for n in range(pairs):
            c = (2 * n + par) * LAT
            ctx_ref[:, c : c + LAT] = out[n * GROUP : (n + 1) * GROUP]

    @pl.when(step == pl.num_programs(1) - 1)
    def _():
        t_ref[...] = total[...].astype(bf16)


def attend(src, q, own, pieces, bias_own, bias_rem):
    rows, width = q.shape
    step_heads = 4
    steps = width // (step_heads * QK)
    keys = NSEL * BLK
    piece_rows = pieces[0].shape[1]
    whole = lambda g, j: (g, 0, 0)
    return pl.pallas_call(
        attend_kernel,
        out_shape=(
            jax.ShapeDtypeStruct((rows, width // QK * LAT), bf16),
            jax.ShapeDtypeStruct((rows, keys), bf16),
        ),
        grid=(2, steps),
        in_specs=[
            smem(),
            pl.BlockSpec((GROUP, step_heads * QK), lambda g, j: (g, j)),
            pl.BlockSpec((None, OWN // 2, PAIR), whole),
        ]
        + [pl.BlockSpec((None, piece_rows, PAIR), whole)] * 8
        + [
            pl.BlockSpec((None, GROUP, OWN), whole),
            pl.BlockSpec((None, 1, keys - OWN), whole),
        ],
        out_specs=(
            pl.BlockSpec((GROUP, step_heads * LAT), lambda g, j: (g, j)),
            pl.BlockSpec((GROUP, keys), lambda g, j: (g, 0)),
        ),
        scratch_shapes=[
            pltpu.VMEM((keys, KW), bf16),
            pltpu.VMEM((keys, KW), bf16),
            pltpu.VMEM((GROUP, keys), f32),
        ],
        compiler_params=params(2),
    )(src, q, own, *pieces, bias_own, bias_rem)


JB = 8


def index_part(iq, keys, b):
    cols = [iq[:, (b * JB + n) * ID : (b * JB + n + 1) * ID] for n in range(JB)]
    return nt(jnp.concatenate(cols, 0), keys)


def logits_kernel(iq_ref, w_ref, own_ref, rem_ref, bias_own, bias_rem, out_ref, keys):
    keys[:OWN] = own_ref[...]
    keys[OWN:] = rem_ref[...]
    rows = iq_ref.shape[0]
    sum_ = jnp.zeros(out_ref.shape, f32)
    for b in range(IH // JB):
        act = index_part(iq_ref, keys[...], b)
        for n in range(JB):
            j = b * JB + n
            sum_ = sum_ + jnp.maximum(act[n * rows : (n + 1) * rows], 0.0) * w_ref[:, j : j + 1]
    logits = sum_ * INDEX_SCALE
    logits = jnp.concatenate(
        [logits[:, :OWN] + bias_own[...], logits[:, OWN:] + bias_rem[...]], 1
    )
    top = jnp.max(logits, -1, keepdims=True)
    shifted = logits - top
    out_ref[...] = shifted - jnp.log(jnp.sum(jnp.exp(shifted), -1, keepdims=True))


def index_specs(rows, heads):
    group = lambda c, h: (h[0] // (heads // 2), 0, 0)
    return group, [
        pl.BlockSpec((rows, IH * ID), lambda c, h: (0, 0)),
        pl.BlockSpec((rows, IH), lambda c, h: (0, 0)),
        pl.BlockSpec((None, OWN, ID), group),
        pl.BlockSpec((NSEL * BLK - OWN, ID), lambda c, h: (0, 0)),
    ]


def index_logits(h, iq, w, own, rem, bias_own, bias_rem, heads):
    rows = iq.shape[0]
    group, specs = index_specs(rows, heads)
    keys = NSEL * BLK

    def kernel(h_ref, *refs):
        logits_kernel(*refs)

    return pl.pallas_call(
        kernel,
        out_shape=jax.ShapeDtypeStruct((rows, keys), f32),
        grid_spec=pltpu.PrefetchScalarGridSpec(
            num_scalar_prefetch=1,
            grid=(1,),
            in_specs=specs
            + [
                pl.BlockSpec((None, rows, OWN), lambda c, h: (h[0], 0, 0)),
                pl.BlockSpec((None, 1, keys - OWN), group),
            ],
            out_specs=pl.BlockSpec((rows, keys), lambda c, h: (0, 0)),
            scratch_shapes=[pltpu.VMEM((keys, ID), bf16)],
        ),
        compiler_params=params(),
    )(h, iq, w, own, rem, bias_own, bias_rem)


def grad_kernel(iq_ref, w_ref, own_ref, rem_ref, logq_ref, part_ref, loss_ref, grad_ref, keys):
    keys[:OWN] = own_ref[...]
    keys[OWN:] = rem_ref[...]
    rows = iq_ref.shape[0]
    target = part_ref[0].astype(f32)
    for n in range(1, part_ref.shape[0]):
        target = target + part_ref[n].astype(f32)
    target = target / H
    log_q = logq_ref[...]
    shown = log_q > 0.5 * NEG
    prob_q = jnp.where(shown, jnp.exp(log_q), 0.0)
    live = shown & (target > 0)
    safe = jnp.where(live, target, 1.0)
    terms = jnp.where(live, target * (jnp.log(safe) - log_q), 0.0)
    loss_ref[...] = jnp.sum(terms, -1, keepdims=True)
    diff = prob_q - target
    for b in range(IH // JB):
        act = index_part(iq_ref, keys[...], b)
        coef = []
        for n in range(JB):
            j = b * JB + n
            value = diff * (w_ref[:, j : j + 1] * INDEX_SCALE)
            coef.append(jnp.where(act[n * rows : (n + 1) * rows] > 0, value, 0.0))
        got = nn(jnp.concatenate(coef, 0).astype(bf16), keys[...])
        for n in range(JB):
            j = b * JB + n
            grad_ref[:, j * ID : (j + 1) * ID] = got[n * rows : (n + 1) * rows]


def index_grads(h, iq, w, own, rem, log_q, parts, heads):
    rows = iq.shape[0]
    group, specs = index_specs(rows, heads)
    keys = NSEL * BLK

    def kernel(h_ref, *refs):
        grad_kernel(*refs)

    return pl.pallas_call(
        kernel,
        out_shape=(
            jax.ShapeDtypeStruct((rows, 1), f32),
            jax.ShapeDtypeStruct((rows, IH * ID), f32),
        ),
        grid_spec=pltpu.PrefetchScalarGridSpec(
            num_scalar_prefetch=1,
            grid=(1,),
            in_specs=specs
            + [
                pl.BlockSpec((rows, keys), lambda c, h: (0, 0)),
                pl.BlockSpec((heads, rows, keys), lambda c, h: (0, 0, 0)),
            ],
            out_specs=(
                pl.BlockSpec((rows, 1), lambda c, h: (0, 0)),
                pl.BlockSpec((rows, IH * ID), lambda c, h: (0, 0)),
            ),
            scratch_shapes=[pltpu.VMEM((keys, ID), bf16)],
        ),
        compiler_params=params(),
    )(h, iq, w, own, rem, log_q, parts)


def gather_head(x, heads):
    ring = [x]
    for d in (2, heads - 2, 4):
        ring.append(lax.ppermute(x, "head", [(i, (i + d) % heads) for i in range(heads)]))
    other = [lax.ppermute(r, "head", [(i, i ^ 1) for i in range(heads)]) for r in ring]
    h = lax.axis_index("head")
    back = jnp.array([0, 2, heads - 2, 4], i32)
    at = jnp.concatenate([h - back + heads, (h ^ 1) - back + heads]) % heads
    return ring + other, at


def body(query, latent, index_keys, index_query, index_weight, block_list, list_len, start):
    seqs = lax.axis_size("seq")
    heads = lax.axis_size("head")
    me = lax.axis_index("seq")
    h = lax.axis_index("head")
    h1 = h.astype(i32).reshape(1)
    blk_dev = latent.shape[0]
    request, place, own_idx = plan(
        me.astype(i32).reshape(1), block_list, list_len, seqs, blk_dev
    )
    asked = lax.all_to_all(request, "seq", split_axis=0, concat_axis=0, tiled=True)
    lat_out, key_out = send(h1, asked.reshape(-1, 1), latent, index_keys, heads)
    lat_in = lax.all_to_all(lat_out, "seq", split_axis=0, concat_axis=0, tiled=True)
    key_in = lax.all_to_all(key_out, "seq", split_axis=0, concat_axis=0, tiled=True)

    own_lat, own_key = own_rows(own_idx, latent, index_keys)
    own_key = own_key.reshape(2, OWN, ID)

    col = jnp.arange(OWN, dtype=i32)
    token = (col % (OWN // 2)) // CAPC * 2 + col // (OWN // 2)
    blocks = jnp.tile(own_idx.reshape(2, CAPC), (1, OWN // CAPC)) + me * blk_dev
    key_pos = blocks * BLK + token[None, :]
    row_pos = start[:, None] + jnp.arange(GROUP, dtype=i32)[None, :]
    bias_own = jnp.where(key_pos[:, None, :] <= row_pos[:, :, None], 0.0, NEG).astype(f32)
    used = jnp.where(place.reshape(2, REM) >= 0, 0.0, NEG).astype(f32)
    bias_rem = jnp.tile(used, (1, BLK))[:, None, :]

    pieces, src = gather_head(pack_lat(place, lat_in), heads)
    rem_key = lax.all_to_all(
        pack_key(place, key_in, heads), "head", split_axis=0, concat_axis=0, tiled=True
    ).reshape(-1, ID)

    context, partial = attend(src, query, own_lat, pieces, bias_own, bias_rem)
    share = index_query.shape[0]
    parts = lax.all_to_all(
        partial.reshape(heads, share, -1), "head", split_axis=0, concat_axis=0, tiled=True
    )
    log_q = index_logits(
        h1, index_query, index_weight, own_key, rem_key,
        bias_own.reshape(heads, share, OWN), bias_rem, heads,
    )
    loss, grad = index_grads(
        h1, index_query, index_weight, own_key, rem_key, log_q, parts, heads
    )
    return context, loss.reshape(-1), grad


def solution(mesh):
    placed = (
        P("seq", "head"),
        P("seq", None),
        P("seq", None),
        P(("seq", "head"), None),
        P(("seq", "head"), None),
        P("seq", None),
        P("seq"),
        P("seq"),
    )
    return jax.shard_map(
        body,
        mesh=mesh,
        in_specs=placed,
        out_specs=(P("seq", "head"), P(("seq", "head")), P(("seq", "head"), None)),
        check_vma=False,
    )
```

```python
import functools
import math

import jax
import jax.numpy as jnp
from jax import lax
from jax.experimental import pallas as pl
from jax.experimental.pallas import tpu as pltpu
from jax.sharding import PartitionSpec as P

H = 128
LAT = 512
IH = 64
ID = 128
BLK = 64
NSEL = 32
GROUP = 128
CAPC = 8
QK = 576

PAIR = 2 * QK
KW = 640
SCALE = 192.0 ** -0.5
INDEX_SCALE = 128.0 ** -0.5
LOG2E = math.log2(math.e)
NEG = -1e30
OWN = CAPC * BLK
PARTS = 1
REM = NSEL - CAPC
VMEM_LIMIT = 56 * 1024 * 1024

f32 = jnp.float32
bf16 = jnp.bfloat16
i32 = jnp.int32


def params(n=1):
    return pltpu.CompilerParams(
        vmem_limit_bytes=VMEM_LIMIT, dimension_semantics=("arbitrary",) * n
    )


def smem():
    return pl.BlockSpec(memory_space=pltpu.SMEM)


def vmem():
    return pl.BlockSpec(memory_space=pltpu.VMEM)


def far(x):
    return pltpu.with_memory_space_constraint(x, pltpu.HBM)


def nt(a, b):
    return lax.dot_general(a, b, (((1,), (1,)), ((), ())), preferred_element_type=f32)


def nn(a, b):
    return jnp.dot(a, b, preferred_element_type=f32)


def plan_kernel(seqs, blk_dev, me_ref, list_ref, len_ref, req_ref, place_ref, own_ref, count):
    cap = 2 * CAPC
    me = me_ref[0]
    req_ref[...] = jnp.full(req_ref.shape, -1, i32)
    for o in range(seqs):
        count[o] = 0
    for n in range(2 * REM):
        place_ref[n] = -1
    for n in range(2 * CAPC):
        own_ref[n] = -1
    for g in range(2):

        def entry(k, carry):
            own_n, rem_n = carry
            block = list_ref[g, k]
            owner = block // blk_dev
            local = block - owner * blk_dev
            mine = owner == me

            @pl.when(mine)
            def _():
                own_ref[g * CAPC + jnp.minimum(own_n, CAPC - 1)] = local

            @pl.when(jnp.logical_not(mine))
            def _():
                rank = jnp.minimum(count[owner], cap - 1)
                count[owner] = rank + 1
                at = owner * cap + rank
                req_ref[pl.ds(at, 1), :] = jnp.full((1, req_ref.shape[1]), local, i32)
                place_ref[g * REM + jnp.minimum(rem_n, REM - 1)] = at

            step = mine.astype(i32)
            return own_n + step, rem_n + 1 - step

        lax.fori_loop(0, len_ref[g], entry, (jnp.int32(0), jnp.int32(0)))


def plan(me, lists, lens, seqs, blk_dev):
    return pl.pallas_call(
        functools.partial(plan_kernel, seqs, blk_dev),
        out_shape=(
            jax.ShapeDtypeStruct((seqs * 2 * CAPC, blk_dev), i32),
            jax.ShapeDtypeStruct((2 * REM,), i32),
            jax.ShapeDtypeStruct((2 * CAPC,), i32),
        ),
        in_specs=[smem()] * 3,
        out_specs=(vmem(), smem(), smem()),
        scratch_shapes=[pltpu.SMEM((seqs,), i32)],
    )(me, lists, lens)


def send_kernel(h_ref, asked_ref, x_ref, out_ref):
    lane = lax.broadcasted_iota(i32, asked_ref.shape, 1)
    pick = (asked_ref[...] == lane).astype(f32).astype(bf16)
    out_ref[...] = nn(pick, x_ref[...]).astype(bf16)


def send(h, asked, x, heads, part, parts):
    rows, blocks = asked.shape
    width = x.shape[1] // heads // parts
    return pl.pallas_call(
        send_kernel,
        out_shape=jax.ShapeDtypeStruct((rows, width), bf16),
        grid_spec=pltpu.PrefetchScalarGridSpec(
            num_scalar_prefetch=1,
            grid=(1,),
            in_specs=[
                pl.BlockSpec((rows, blocks), lambda c, h: (0, 0)),
                pl.BlockSpec((blocks, width), lambda c, h: (0, h[0] * parts + part)),
            ],
            out_specs=pl.BlockSpec((rows, width), lambda c, h: (0, 0)),
        ),
        compiler_params=params(),
    )(h, asked, far(x))


def picker(idx_ref, rows, width):
    row = lax.broadcasted_iota(i32, (rows, width), 0)
    lane = lax.broadcasted_iota(i32, (rows, width), 1)
    want = jnp.full((rows, width), -1, i32)
    for r in range(rows):
        want = jnp.where(row == r, idx_ref[r], want)
    return (want == lane).astype(f32).astype(bf16)


def own_kernel(idx_ref, lat_ref, key_ref, lat_out, key_out):
    pick = picker(idx_ref, 2 * CAPC, lat_ref.shape[0])
    pairs = lat_ref.shape[1] // PAIR
    got = [nn(pick, lat_ref[:, i * PAIR : (i + 1) * PAIR]) for i in range(pairs)]
    for g in range(2):
        part = [x[g * CAPC : (g + 1) * CAPC] for x in got]
        lat_out[g] = jnp.concatenate(part, 0).astype(bf16)
    got = [nn(pick, key_ref[:, t * ID : (t + 1) * ID]) for t in range(2 * pairs)]
    for g in range(2):
        for par in range(2):
            part = [x[g * CAPC : (g + 1) * CAPC] for x in got[par::2]]
            key_out[g, par] = jnp.concatenate(part, 0).astype(bf16)


def own_rows(idx, latent, keys):
    blocks = latent.shape[0]
    steps = 8
    pairs = BLK // 2 // steps
    rows = pairs * CAPC
    return pl.pallas_call(
        own_kernel,
        out_shape=(
            jax.ShapeDtypeStruct((2, OWN // 2, PAIR), bf16),
            jax.ShapeDtypeStruct((2, 2, OWN // 2, ID), bf16),
        ),
        grid=(steps,),
        in_specs=[
            smem(),
            pl.BlockSpec((blocks, pairs * PAIR), lambda c: (0, c)),
            pl.BlockSpec((blocks, 2 * pairs * ID), lambda c: (0, c)),
        ],
        out_specs=(
            pl.BlockSpec((2, rows, PAIR), lambda c: (0, c, 0)),
            pl.BlockSpec((2, 2, rows, ID), lambda c: (0, 0, c, 0)),
        ),
        compiler_params=params(),
    )(idx, far(latent), far(keys))


def pack_lat_kernel(idx_ref, lat_ref, lat_out):
    pick = picker(idx_ref, 2 * REM, lat_ref.shape[0])
    pairs = lat_ref.shape[1] // PAIR
    got = [nn(pick, lat_ref[:, i * PAIR : (i + 1) * PAIR]) for i in range(pairs)]
    for g in range(2):
        part = [x[g * REM : (g + 1) * REM] for x in got]
        lat_out[g] = jnp.concatenate(part, 0).astype(bf16)


def pack_lat(idx, lat):
    pairs = lat.shape[1] // PAIR
    return pl.pallas_call(
        pack_lat_kernel,
        out_shape=jax.ShapeDtypeStruct((2, pairs * REM, PAIR), bf16),
        in_specs=[smem(), vmem()],
        out_specs=vmem(),
        compiler_params=params(0),
    )(idx, lat)


def part_pairs(tokens, c):
    pairs = tokens // 2 // PARTS
    return range(c * pairs, (c + 1) * pairs)


def pack_key_kernel(idx_ref, key_ref, key_out):
    pick = picker(idx_ref, 2 * REM, key_ref.shape[0])
    heads = key_out.shape[0]
    tokens = key_ref.shape[1] // ID
    got = [nn(pick, key_ref[:, t * ID : (t + 1) * ID]) for t in range(tokens)]
    for g in range(2):
        order = [2 * i + par for c in range(PARTS) for par in range(2) for i in part_pairs(tokens, c)]
        part = [got[t][g * REM : (g + 1) * REM] for t in order]
        rows = jnp.concatenate(part, 0).astype(bf16)
        for d in range(heads // 2):
            key_out[g * (heads // 2) + d] = rows


def pack_key(idx, keys, heads):
    tokens = keys.shape[1] // ID
    return pl.pallas_call(
        pack_key_kernel,
        out_shape=jax.ShapeDtypeStruct((heads, tokens * REM, ID), bf16),
        in_specs=[smem(), vmem()],
        out_specs=vmem(),
        compiler_params=params(0),
    )(idx, keys)


def place_keys(x, ka, kb, at, rows):
    xf = x.astype(f32)
    lane = lax.broadcasted_iota(i32, (rows, KW), 1)
    gap = KW - QK
    even = jnp.where(lane < QK, xf[:, :KW], 0.0)
    odd = jnp.where(lane >= gap, xf[:, PAIR - KW :], 0.0)
    ka[pl.ds(at, rows), :] = even.astype(bf16)
    kb[pl.ds(at, rows), :] = pltpu.roll(even, gap, 1).astype(bf16)
    kb[pl.ds(at + rows, rows), :] = odd.astype(bf16)
    ka[pl.ds(at + rows, rows), :] = pltpu.roll(odd, QK, 1).astype(bf16)


def score(q, keys, bias, par):
    pairs = q.shape[1] // PAIR
    first = [n * PAIR + par * (PAIR - KW) for n in range(pairs)]
    rows = jnp.concatenate([q[:, c : c + KW] for c in first], 0)
    s = nt(rows, keys)
    if bias.shape[0] > 1:
        s = (s.reshape(pairs, *bias.shape) + bias).reshape(s.shape)
    else:
        s = s + bias
    top = jnp.max(s, -1, keepdims=True)
    w = jnp.exp2((s - top) * (SCALE * LOG2E))
    return w, top, jnp.sum(w, -1, keepdims=True)


def lane_rows(x):
    eye = lax.broadcasted_iota(i32, (GROUP, GROUP), 0) == lax.broadcasted_iota(i32, (GROUP, GROUP), 1)
    parts = [x[r : r + GROUP] for r in range(0, x.shape[0], GROUP)]
    return jnp.concatenate(
        [jnp.sum(jnp.where(eye, part, 0.0), 0, keepdims=True) for part in parts], 0
    )


def column(rows):
    eye = lax.broadcasted_iota(i32, (GROUP, GROUP), 0) == lax.broadcasted_iota(i32, (GROUP, GROUP), 1)
    parts = [rows[n : n + 1] for n in range(rows.shape[0])]
    return jnp.concatenate(
        [jnp.sum(jnp.where(eye, part, 0.0), 1, keepdims=True) for part in parts], 0
    )


HEAD_ROWS = 16


def own_stage_kernel(q_ref, own_ref, bias_ref, p_ref, st_ref, v_ref, ka, kb):
    place_keys(own_ref[...], ka, kb, 0, own_ref.shape[0])
    v_ref[...] = ka[:, :LAT]
    q, bias = q_ref[...], bias_ref[...]
    n = st_ref.shape[0] // 4
    for par, keys in ((0, ka), (1, kb)):
        w, top, sum_ = score(q, keys[...], bias, par)
        p_ref[par] = w.astype(bf16)
        st_ref[par * n : (par + 1) * n] = lane_rows(top)
        st_ref[(par + 2) * n : (par + 3) * n] = lane_rows(sum_)


def anywhere():
    return pl.BlockSpec(memory_space=pl.ANY)


def group_spec(*shape):
    return pl.BlockSpec((None, *shape), lambda g: (g, *[0] * len(shape)))


def rows_spec(width):
    return pl.BlockSpec((GROUP, width), lambda g: (g, 0))


def own_stage(q, own, bias):
    heads = q.shape[1] // QK
    tall = heads // 2 * GROUP
    return pl.pallas_call(
        own_stage_kernel,
        out_shape=(
            jax.ShapeDtypeStruct((2, 2, tall, OWN), bf16),
            jax.ShapeDtypeStruct((2, 2 * heads, GROUP), f32),
            jax.ShapeDtypeStruct((2, OWN, LAT), bf16),
        ),
        grid=(2,),
        in_specs=[rows_spec(q.shape[1]), group_spec(*own.shape[1:]), group_spec(GROUP, OWN)],
        out_specs=(
            group_spec(2, tall, OWN),
            group_spec(2 * heads, GROUP),
            group_spec(OWN, LAT),
        ),
        scratch_shapes=[pltpu.VMEM((OWN, KW), bf16)] * 2,
        compiler_params=params(1),
    )(far(q), own, bias)


def rest_kernel(n, *refs):
    src_ref, q_ref, pieces, refs = refs[0], refs[1], refs[2 : 2 + n], refs[2 + n :]
    bias_ref, po_ref, st_ref, p_ref, f_ref, v_ref, t_ref = refs[:7]
    ka, kb, ps, total, factors, sem = refs[7:]
    g = pl.program_id(0)
    for k, piece in enumerate(pieces):
        rows = piece.shape[1]
        at = pl.multiple_of(src_ref[k] * (2 * rows), 2 * rows)
        place_keys(piece[g], ka, kb, at, rows)
    v_ref[...] = ka[:, :LAT]
    q, bias = q_ref[...], bias_ref[...]
    n = st_ref.shape[0] // 4
    tall = n * GROUP
    c = SCALE * LOG2E

    def out_copy(group, par):
        return pltpu.make_async_copy(
            ps.at[group, par], p_ref.at[group, par], sem.at[group * 2 + par]
        )

    for par, keys in ((0, ka), (1, kb)):
        w, top, sum_ = score(q, keys[...], bias, par)
        ps[g, par] = w.astype(bf16)
        out_copy(g, par).start()
        top_o = column(st_ref[par * n : (par + 1) * n])
        sum_o = column(st_ref[(par + 2) * n : (par + 3) * n])
        most = jnp.maximum(top_o, top)
        fs = [jnp.exp2((x - most) * c) for x in (top_o, top)]
        inv = 1.0 / (fs[0] * sum_o + fs[1] * sum_)
        for k in range(2):
            f = fs[k] * inv
            factors[:, k : k + 1] = f
            f_ref[(2 * k + par) * n : (2 * k + par + 1) * n] = lane_rows(f)
        for r in range(0, GROUP, HEAD_ROWS):
            at = 0
            for k, x in enumerate((po_ref.at[par], ps.at[g, par])):
                wide = x.shape[1]
                add = total[r : r + HEAD_ROWS, at : at + wide] if par else 0.0
                for d in range(r, tall, GROUP):
                    f = factors[d : d + HEAD_ROWS, k : k + 1]
                    add = add + x[d : d + HEAD_ROWS, :].astype(f32) * f
                if par:
                    t_ref[r : r + HEAD_ROWS, at : at + wide] = add.astype(bf16)
                else:
                    total[r : r + HEAD_ROWS, at : at + wide] = add
                at += wide

    @pl.when(g == 1)
    def _():
        for group in range(2):
            for par in range(2):
                out_copy(group, par).wait()


def rest_stage(q, src, pieces, bias, own):
    heads = q.shape[1] // QK
    tall = heads // 2 * GROUP
    keys = bias.shape[2]
    every = NSEL * BLK
    return pl.pallas_call(
        functools.partial(rest_kernel, len(pieces)),
        out_shape=(
            jax.ShapeDtypeStruct((2, 2, tall, keys), bf16),
            jax.ShapeDtypeStruct((2, 2 * heads, GROUP), f32),
            jax.ShapeDtypeStruct((2, keys, LAT), bf16),
            jax.ShapeDtypeStruct((q.shape[0], every), bf16),
        ),
        grid=(2,),
        in_specs=[smem(), rows_spec(q.shape[1])]
        + [vmem() for x in pieces]
        + [group_spec(1, keys), group_spec(2, tall, OWN), group_spec(2 * heads, GROUP)],
        out_specs=(
            anywhere(),
            group_spec(2 * heads, GROUP),
            group_spec(keys, LAT),
            rows_spec(every),
        ),
        scratch_shapes=[
            pltpu.VMEM((keys, KW), bf16),
            pltpu.VMEM((keys, KW), bf16),
            pltpu.VMEM((2, 2, tall, keys), bf16),
            pltpu.VMEM((GROUP, every), f32),
            pltpu.VMEM((tall, GROUP), f32),
            pltpu.SemaphoreType.DMA((4,)),
        ],
        compiler_params=params(1),
    )(src, far(q), *pieces, bias, far(own[0]), own[1])


def context_kernel(f_ref, po_ref, pr_ref, vo_ref, vr_ref, ctx_ref):
    par = pl.program_id(1)
    n = f_ref.shape[0] // 4
    fs = [column(f_ref[pl.ds(pl.multiple_of((2 * k + par) * n, n), n), :]) for k in range(2)]
    out = nn(po_ref[...], vo_ref[...]) * fs[0] + nn(pr_ref[...], vr_ref[...]) * fs[1]
    out = out.astype(bf16)
    for k in range(n):
        at = pl.multiple_of((2 * k + par) * LAT, LAT)
        ctx_ref[:, pl.ds(at, LAT)] = out[k * GROUP : (k + 1) * GROUP]


def contexts(f, po, pr, vo, vr):
    heads = f.shape[1] // 2
    part = lambda x: pl.BlockSpec((None, None, *x.shape[2:]), lambda g, par: (g, par, 0, 0))
    group = lambda x: pl.BlockSpec((None, *x.shape[1:]), lambda g, par: (g, 0, 0))
    return pl.pallas_call(
        context_kernel,
        out_shape=jax.ShapeDtypeStruct((2 * GROUP, heads * LAT), bf16),
        grid=(2, 2),
        in_specs=[group(f), part(po), part(pr), group(vo), group(vr)],
        out_specs=pl.BlockSpec((GROUP, heads * LAT), lambda g, par: (g, 0)),
        compiler_params=params(2),
    )(f, far(po), far(pr), vo, vr)


JB = 8


def index_part(iq, keys, b):
    cols = [iq[:, (b * JB + n) * ID : (b * JB + n + 1) * ID] for n in range(JB)]
    return nt(jnp.concatenate(cols, 0), keys)


def fill_index_keys(own_ref, rem_ref, keys):
    keys[:OWN] = own_ref[...]
    heads, parts, rows = rem_ref.shape[:3]
    for c in range(parts):
        for d in range(heads):
            at = OWN + (c * heads + d) * rows
            keys[at : at + rows] = rem_ref[d, c]


def logits_kernel(iq_ref, w_ref, own_ref, rem_ref, bias_own, bias_rem, out_ref, keys):
    fill_index_keys(own_ref, rem_ref, keys)
    rows = iq_ref.shape[0]
    sum_ = jnp.zeros(out_ref.shape, f32)
    for b in range(IH // JB):
        act = index_part(iq_ref, keys[...], b)
        for n in range(JB):
            j = b * JB + n
            sum_ = sum_ + jnp.maximum(act[n * rows : (n + 1) * rows], 0.0) * w_ref[:, j : j + 1]
    logits = sum_ * INDEX_SCALE
    rem = jnp.concatenate([bias_rem[...]] * PARTS, 1)
    logits = jnp.concatenate([logits[:, :OWN] + bias_own[...], logits[:, OWN:] + rem], 1)
    top = jnp.max(logits, -1, keepdims=True)
    shifted = logits - top
    out_ref[...] = shifted - jnp.log(jnp.sum(jnp.exp(shifted), -1, keepdims=True))


def index_specs(rows, heads, rem):
    group = lambda c, h: (h[0] // (heads // 2), 0, 0)
    return group, [
        pl.BlockSpec((rows, IH * ID), lambda c, h: (0, 0)),
        pl.BlockSpec((rows, IH), lambda c, h: (0, 0)),
        pl.BlockSpec((None, OWN, ID), group),
        pl.BlockSpec(rem.shape, lambda c, h: (0, 0, 0, 0)),
    ]


def index_logits(h, iq, w, own, rem, bias_own, bias_rem, heads):
    rows = iq.shape[0]
    group, specs = index_specs(rows, heads, rem)
    keys = NSEL * BLK

    def kernel(h_ref, *refs):
        logits_kernel(*refs)

    return pl.pallas_call(
        kernel,
        out_shape=jax.ShapeDtypeStruct((rows, keys), f32),
        grid_spec=pltpu.PrefetchScalarGridSpec(
            num_scalar_prefetch=1,
            grid=(1,),
            in_specs=specs
            + [
                pl.BlockSpec((None, rows, OWN), lambda c, h: (h[0], 0, 0)),
                pl.BlockSpec((None, 1, bias_rem.shape[2]), group),
            ],
            out_specs=pl.BlockSpec((rows, keys), lambda c, h: (0, 0)),
            scratch_shapes=[pltpu.VMEM((keys, ID), bf16)],
        ),
        compiler_params=params(),
    )(h, iq, w, own, rem, bias_own, bias_rem)


def grad_kernel(iq_ref, w_ref, own_ref, rem_ref, logq_ref, part_ref, loss_ref, grad_ref, keys):
    fill_index_keys(own_ref, rem_ref, keys)
    rows = iq_ref.shape[0]
    target = part_ref[0].astype(f32)
    for n in range(1, part_ref.shape[0]):
        target = target + part_ref[n].astype(f32)
    target = target / H
    log_q = logq_ref[...]
    shown = log_q > 0.5 * NEG
    prob_q = jnp.where(shown, jnp.exp(log_q), 0.0)
    live = shown & (target > 0)
    safe = jnp.where(live, target, 1.0)
    terms = jnp.where(live, target * (jnp.log(safe) - log_q), 0.0)
    loss_ref[...] = jnp.sum(terms, -1, keepdims=True)
    diff = prob_q - target
    for b in range(IH // JB):
        act = index_part(iq_ref, keys[...], b)
        coef = []
        for n in range(JB):
            j = b * JB + n
            value = diff * (w_ref[:, j : j + 1] * INDEX_SCALE)
            coef.append(jnp.where(act[n * rows : (n + 1) * rows] > 0, value, 0.0))
        got = nn(jnp.concatenate(coef, 0).astype(bf16), keys[...])
        for n in range(JB):
            j = b * JB + n
            grad_ref[:, j * ID : (j + 1) * ID] = got[n * rows : (n + 1) * rows]


def index_grads(h, iq, w, own, rem, log_q, parts, heads):
    rows = iq.shape[0]
    group, specs = index_specs(rows, heads, rem)
    keys = NSEL * BLK

    def kernel(h_ref, *refs):
        grad_kernel(*refs)

    return pl.pallas_call(
        kernel,
        out_shape=(
            jax.ShapeDtypeStruct((rows, 1), f32),
            jax.ShapeDtypeStruct((rows, IH * ID), f32),
        ),
        grid_spec=pltpu.PrefetchScalarGridSpec(
            num_scalar_prefetch=1,
            grid=(1,),
            in_specs=specs
            + [
                pl.BlockSpec((rows, keys), lambda c, h: (0, 0)),
                pl.BlockSpec((heads, rows, keys), lambda c, h: (0, 0, 0)),
            ],
            out_specs=(
                pl.BlockSpec((rows, 1), lambda c, h: (0, 0)),
                pl.BlockSpec((rows, IH * ID), lambda c, h: (0, 0)),
            ),
            scratch_shapes=[pltpu.VMEM((keys, ID), bf16)],
        ),
        compiler_params=params(),
    )(h, iq, w, own, rem, log_q, parts)


def gather_head(x, heads):
    ring = [x]
    for d in (2, heads - 2, 4):
        ring.append(lax.ppermute(x, "head", [(i, (i + d) % heads) for i in range(heads)]))
    other = [lax.ppermute(r, "head", [(i, i ^ 1) for i in range(heads)]) for r in ring]
    h = lax.axis_index("head")
    back = jnp.array([0, 2, heads - 2, 4], i32)
    at = jnp.concatenate([h - back + heads, (h ^ 1) - back + heads]) % heads
    return ring + other, at


def after(x, *first):
    return lax.optimization_barrier((x, *first))[0]


def swap(x, axis):
    return lax.all_to_all(x, axis, split_axis=0, concat_axis=0, tiled=True)


def body(query, latent, index_keys, index_query, index_weight, block_list, list_len, start):
    seqs = lax.axis_size("seq")
    heads = lax.axis_size("head")
    me = lax.axis_index("seq")
    h = lax.axis_index("head")
    h1 = h.astype(i32).reshape(1)
    blk_dev = latent.shape[0]
    request, place, own_idx = plan(
        me.astype(i32).reshape(1), block_list, list_len, seqs, blk_dev
    )
    asked = swap(request, "seq")
    out_l = send(h1, asked, latent, heads, 0, 1)
    in_l = swap(out_l, "seq")
    out_k = send(h1, after(asked, out_l), index_keys, heads, 0, 1)
    own_lat, own_key = own_rows(after(own_idx, out_k), latent, index_keys)
    own_key = own_key.reshape(2, OWN, ID)

    col = jnp.arange(OWN, dtype=i32)
    token = (col % (OWN // 2)) // CAPC * 2 + col // (OWN // 2)
    blocks = jnp.tile(own_idx.reshape(2, CAPC), (1, OWN // CAPC)) + me * blk_dev
    key_pos = blocks * BLK + token[None, :]
    row_pos = start[:, None] + jnp.arange(GROUP, dtype=i32)[None, :]
    bias_own = jnp.where(key_pos[:, None, :] <= row_pos[:, :, None], 0.0, NEG).astype(f32)
    used = jnp.where(place.reshape(2, REM) >= 0, 0.0, NEG).astype(f32)
    bias_rem = jnp.tile(used, (1, BLK // PARTS))[:, None, :]

    own = own_stage(query, own_lat, bias_own)
    in_l = after(in_l, own[0], bias_rem)
    packed = pack_lat(place, in_l)
    pieces, src = gather_head(packed, heads)
    in_k = swap(after(out_k, packed), "seq")
    packed_k = pack_key(place, in_k, heads)
    rem_key = swap(packed_k, "head").reshape(heads, PARTS, -1, ID)
    p_r, factors, v_r, partial = rest_stage(after(query, packed_k), src, pieces, bias_rem, own)
    share = index_query.shape[0]
    parts = swap(partial.reshape(heads, share, -1), "head")
    context = contexts(after(factors, partial), own[0], p_r, own[2], v_r)
    log_q = index_logits(
        h1, index_query, index_weight, own_key, rem_key,
        bias_own.reshape(heads, share, OWN), bias_rem, heads,
    )
    parts = after(parts, context, log_q)
    loss, grad = index_grads(
        h1, index_query, index_weight, own_key, rem_key, log_q, parts, heads
    )
    return context, loss.reshape(-1), grad


def solution(mesh):
    placed = (
        P("seq", "head"),
        P("seq", None),
        P("seq", None),
        P(("seq", "head"), None),
        P(("seq", "head"), None),
        P("seq", None),
        P("seq"),
        P("seq"),
    )
    return jax.shard_map(
        body,
        mesh=mesh,
        in_specs=placed,
        out_specs=(P("seq", "head"), P(("seq", "head")), P(("seq", "head"), None)),
        check_vma=False,
    )
```

```python
import functools
import math

import jax
import jax.numpy as jnp
from jax import lax
from jax.experimental import pallas as pl
from jax.experimental.pallas import tpu as pltpu
from jax.sharding import PartitionSpec as P

H = 128
LAT = 512
IH = 64
ID = 128
BLK = 64
NSEL = 32
GROUP = 128
CAPC = 8
QK = 576

PAIR = 2 * QK
KW = 640
SCALE = 192.0 ** -0.5
INDEX_SCALE = 128.0 ** -0.5
LOG2E = math.log2(math.e)
NEG = -1e30
OWN = CAPC * BLK
PARTS = 1
REM = NSEL - CAPC
VMEM_LIMIT = 56 * 1024 * 1024

f32 = jnp.float32
bf16 = jnp.bfloat16
i32 = jnp.int32


def params(n=1):
    return pltpu.CompilerParams(
        vmem_limit_bytes=VMEM_LIMIT, dimension_semantics=("arbitrary",) * n
    )


def smem():
    return pl.BlockSpec(memory_space=pltpu.SMEM)


def vmem():
    return pl.BlockSpec(memory_space=pltpu.VMEM)


def far(x):
    return pltpu.with_memory_space_constraint(x, pltpu.HBM)


def near(x):
    return pltpu.with_memory_space_constraint(x, pltpu.VMEM)


def nt(a, b):
    return lax.dot_general(a, b, (((1,), (1,)), ((), ())), preferred_element_type=f32)


def nn(a, b):
    return jnp.dot(a, b, preferred_element_type=f32)


def plan_kernel(seqs, blk_dev, me_ref, list_ref, len_ref, req_ref, place_ref, own_ref, count):
    cap = 2 * CAPC
    me = me_ref[0]
    req_ref[...] = jnp.full(req_ref.shape, -1, i32)
    for o in range(seqs):
        count[o] = 0
    for n in range(2 * REM):
        place_ref[n] = -1
    for n in range(2 * CAPC):
        own_ref[n] = -1
    for g in range(2):

        def entry(k, carry):
            own_n, rem_n = carry
            block = list_ref[g, k]
            owner = block // blk_dev
            local = block - owner * blk_dev
            mine = owner == me

            @pl.when(mine)
            def _():
                own_ref[g * CAPC + jnp.minimum(own_n, CAPC - 1)] = local

            @pl.when(jnp.logical_not(mine))
            def _():
                rank = jnp.minimum(count[owner], cap - 1)
                count[owner] = rank + 1
                at = owner * cap + rank
                req_ref[pl.ds(at, 1), :] = jnp.full((1, req_ref.shape[1]), local, i32)
                place_ref[g * REM + jnp.minimum(rem_n, REM - 1)] = at

            step = mine.astype(i32)
            return own_n + step, rem_n + 1 - step

        lax.fori_loop(0, len_ref[g], entry, (jnp.int32(0), jnp.int32(0)))


def plan(me, lists, lens, seqs, blk_dev):
    return pl.pallas_call(
        functools.partial(plan_kernel, seqs, blk_dev),
        out_shape=(
            jax.ShapeDtypeStruct((seqs * 2 * CAPC, blk_dev), i32),
            jax.ShapeDtypeStruct((2 * REM,), i32),
            jax.ShapeDtypeStruct((2 * CAPC,), i32),
        ),
        in_specs=[smem()] * 3,
        out_specs=(vmem(), smem(), smem()),
        scratch_shapes=[pltpu.SMEM((seqs,), i32)],
    )(me, lists, lens)


def send_kernel(h_ref, asked_ref, x_ref, out_ref):
    lane = lax.broadcasted_iota(i32, asked_ref.shape, 1)
    pick = (asked_ref[...] == lane).astype(f32).astype(bf16)
    out_ref[...] = nn(pick, x_ref[...]).astype(bf16)


def send(h, asked, x, heads, part, parts):
    rows, blocks = asked.shape
    width = x.shape[1] // heads // parts
    return pl.pallas_call(
        send_kernel,
        out_shape=jax.ShapeDtypeStruct((rows, width), bf16),
        grid_spec=pltpu.PrefetchScalarGridSpec(
            num_scalar_prefetch=1,
            grid=(1,),
            in_specs=[
                pl.BlockSpec((rows, blocks), lambda c, h: (0, 0)),
                pl.BlockSpec((blocks, width), lambda c, h: (0, h[0] * parts + part)),
            ],
            out_specs=pl.BlockSpec((rows, width), lambda c, h: (0, 0)),
        ),
        compiler_params=params(),
    )(h, near(asked), far(x))


def picker(idx_ref, rows, width):
    row = lax.broadcasted_iota(i32, (rows, width), 0)
    lane = lax.broadcasted_iota(i32, (rows, width), 1)
    want = jnp.full((rows, width), -1, i32)
    for r in range(rows):
        want = jnp.where(row == r, idx_ref[r], want)
    return (want == lane).astype(f32).astype(bf16)


def own_kernel(idx_ref, lat_ref, key_ref, lat_out, key_out):
    pick = picker(idx_ref, 2 * CAPC, lat_ref.shape[0])
    pairs = lat_ref.shape[1] // PAIR
    got = [nn(pick, lat_ref[:, i * PAIR : (i + 1) * PAIR]) for i in range(pairs)]
    for g in range(2):
        part = [x[g * CAPC : (g + 1) * CAPC] for x in got]
        lat_out[g] = jnp.concatenate(part, 0).astype(bf16)
    got = [nn(pick, key_ref[:, t * ID : (t + 1) * ID]) for t in range(2 * pairs)]
    for g in range(2):
        for par in range(2):
            part = [x[g * CAPC : (g + 1) * CAPC] for x in got[par::2]]
            key_out[g, par] = jnp.concatenate(part, 0).astype(bf16)


def own_rows(idx, latent, keys):
    blocks = latent.shape[0]
    steps = 8
    pairs = BLK // 2 // steps
    rows = pairs * CAPC
    return pl.pallas_call(
        own_kernel,
        out_shape=(
            jax.ShapeDtypeStruct((2, OWN // 2, PAIR), bf16),
            jax.ShapeDtypeStruct((2, 2, OWN // 2, ID), bf16),
        ),
        grid=(steps,),
        in_specs=[
            smem(),
            pl.BlockSpec((blocks, pairs * PAIR), lambda c: (0, c)),
            pl.BlockSpec((blocks, 2 * pairs * ID), lambda c: (0, c)),
        ],
        out_specs=(
            pl.BlockSpec((2, rows, PAIR), lambda c: (0, c, 0)),
            pl.BlockSpec((2, 2, rows, ID), lambda c: (0, 0, c, 0)),
        ),
        compiler_params=params(),
    )(idx, far(latent), far(keys))


def pack_lat_kernel(idx_ref, lat_ref, lat_out):
    pick = picker(idx_ref, 2 * REM, lat_ref.shape[0])
    pairs = lat_ref.shape[1] // PAIR
    got = [nn(pick, lat_ref[:, i * PAIR : (i + 1) * PAIR]) for i in range(pairs)]
    for g in range(2):
        part = [x[g * REM : (g + 1) * REM] for x in got]
        lat_out[g] = jnp.concatenate(part, 0).astype(bf16)


def pack_lat(idx, lat):
    pairs = lat.shape[1] // PAIR
    return pl.pallas_call(
        pack_lat_kernel,
        out_shape=jax.ShapeDtypeStruct((2, pairs * REM, PAIR), bf16),
        in_specs=[smem(), vmem()],
        out_specs=vmem(),
        compiler_params=params(0),
    )(idx, near(lat))


def part_pairs(tokens, c):
    pairs = tokens // 2 // PARTS
    return range(c * pairs, (c + 1) * pairs)


def pack_key_kernel(idx_ref, key_ref, key_out):
    pick = picker(idx_ref, 2 * REM, key_ref.shape[0])
    tokens = key_ref.shape[1] // ID
    got = [nn(pick, key_ref[:, t * ID : (t + 1) * ID]) for t in range(tokens)]
    for g in range(2):
        order = [2 * i + par for c in range(PARTS) for par in range(2) for i in part_pairs(tokens, c)]
        part = [got[t][g * REM : (g + 1) * REM] for t in order]
        rows = jnp.concatenate(part, 0).astype(bf16)
        key_out[g] = rows


def pack_key(idx, keys):
    tokens = keys.shape[1] // ID
    return pl.pallas_call(
        pack_key_kernel,
        out_shape=jax.ShapeDtypeStruct((2, tokens * REM, ID), bf16),
        in_specs=[smem(), vmem()],
        out_specs=vmem(),
        compiler_params=params(0),
    )(idx, near(keys))


def place_keys(x, ka, kb, at, rows):
    xf = x.astype(f32)
    lane = lax.broadcasted_iota(i32, (rows, KW), 1)
    gap = KW - QK
    even = jnp.where(lane < QK, xf[:, :KW], 0.0)
    odd = jnp.where(lane >= gap, xf[:, PAIR - KW :], 0.0)
    ka[pl.ds(at, rows), :] = even.astype(bf16)
    kb[pl.ds(at, rows), :] = pltpu.roll(even, gap, 1).astype(bf16)
    kb[pl.ds(at + rows, rows), :] = odd.astype(bf16)
    ka[pl.ds(at + rows, rows), :] = pltpu.roll(odd, QK, 1).astype(bf16)


def score(q, keys, bias, par):
    pairs = q.shape[1] // PAIR
    first = [n * PAIR + par * (PAIR - KW) for n in range(pairs)]
    rows = jnp.concatenate([q[:, c : c + KW] for c in first], 0)
    s = nt(rows, keys)
    if bias.shape[0] > 1:
        s = (s.reshape(pairs, *bias.shape) + bias).reshape(s.shape)
    else:
        s = s + bias
    top = jnp.max(s, -1, keepdims=True)
    w = jnp.exp2((s - top) * (SCALE * LOG2E))
    return w, top, jnp.sum(w, -1, keepdims=True)


def lane_rows(x):
    eye = lax.broadcasted_iota(i32, (GROUP, GROUP), 0) == lax.broadcasted_iota(i32, (GROUP, GROUP), 1)
    parts = [x[r : r + GROUP] for r in range(0, x.shape[0], GROUP)]
    return jnp.concatenate(
        [jnp.sum(jnp.where(eye, part, 0.0), 0, keepdims=True) for part in parts], 0
    )


def column(rows):
    eye = lax.broadcasted_iota(i32, (GROUP, GROUP), 0) == lax.broadcasted_iota(i32, (GROUP, GROUP), 1)
    parts = [rows[n : n + 1] for n in range(rows.shape[0])]
    return jnp.concatenate(
        [jnp.sum(jnp.where(eye, part, 0.0), 1, keepdims=True) for part in parts], 0
    )


HEAD_ROWS = 16


def own_stage_kernel(q_ref, own_ref, bias_ref, p_ref, st_ref, v_ref, ka, kb):
    place_keys(own_ref[...], ka, kb, 0, own_ref.shape[0])
    v_ref[...] = ka[:, :LAT]
    q, bias = q_ref[...], bias_ref[...]
    n = st_ref.shape[0] // 4
    for par, keys in ((0, ka), (1, kb)):
        w, top, sum_ = score(q, keys[...], bias, par)
        p_ref[par] = w.astype(bf16)
        st_ref[par * n : (par + 1) * n] = lane_rows(top)
        st_ref[(par + 2) * n : (par + 3) * n] = lane_rows(sum_)


def anywhere():
    return pl.BlockSpec(memory_space=pl.ANY)


def group_spec(*shape):
    return pl.BlockSpec((None, *shape), lambda g: (g, *[0] * len(shape)))


def rows_spec(width):
    return pl.BlockSpec((GROUP, width), lambda g: (g, 0))


def own_stage(q, own, bias):
    heads = q.shape[1] // QK
    tall = heads // 2 * GROUP
    return pl.pallas_call(
        own_stage_kernel,
        out_shape=(
            jax.ShapeDtypeStruct((2, 2, tall, OWN), bf16),
            jax.ShapeDtypeStruct((2, 2 * heads, GROUP), f32),
            jax.ShapeDtypeStruct((2, OWN, LAT), bf16),
        ),
        grid=(2,),
        in_specs=[rows_spec(q.shape[1]), group_spec(*own.shape[1:]), group_spec(GROUP, OWN)],
        out_specs=(
            group_spec(2, tall, OWN),
            group_spec(2 * heads, GROUP),
            group_spec(OWN, LAT),
        ),
        scratch_shapes=[pltpu.VMEM((OWN, KW), bf16)] * 2,
        compiler_params=params(1),
    )(far(q), own, bias)


def rest_kernel(n, *refs):
    src_ref, q_ref, pieces, refs = refs[0], refs[1], refs[2 : 2 + n], refs[2 + n :]
    bias_ref, po_ref, st_ref, key_ref, p_ref, f_ref, v_ref, t_ref = refs[:8]
    ka, kb, ps, total, factors, sem = refs[8:]
    g = pl.program_id(0)
    for k, piece in enumerate(pieces):
        rows = piece.shape[1]
        at = pl.multiple_of(src_ref[k] * (2 * rows), 2 * rows)
        place_keys(piece[g], ka, kb, at, rows)
    v_ref[...] = ka[:, :LAT]
    q, bias = q_ref[...], bias_ref[...]
    n = st_ref.shape[0] // 4
    tall = n * GROUP
    c = SCALE * LOG2E

    def out_copy(group, par):
        return pltpu.make_async_copy(
            ps.at[group, par], p_ref.at[group, par], sem.at[group * 2 + par]
        )

    for par, keys in ((0, ka), (1, kb)):
        w, top, sum_ = score(q, keys[...], bias, par)
        ps[g, par] = w.astype(bf16)
        out_copy(g, par).start()
        top_o = column(st_ref[par * n : (par + 1) * n])
        sum_o = column(st_ref[(par + 2) * n : (par + 3) * n])
        most = jnp.maximum(top_o, top)
        fs = [jnp.exp2((x - most) * c) for x in (top_o, top)]
        inv = 1.0 / (fs[0] * sum_o + fs[1] * sum_)
        for k in range(2):
            f = fs[k] * inv
            factors[:, k : k + 1] = f
            f_ref[(2 * k + par) * n : (2 * k + par + 1) * n] = lane_rows(f)
        for r in range(0, GROUP, HEAD_ROWS):
            at = 0
            for k, x in enumerate((po_ref.at[par], ps.at[g, par])):
                wide = x.shape[1]
                add = total[r : r + HEAD_ROWS, at : at + wide] if par else 0.0
                for d in range(r, tall, GROUP):
                    f = factors[d : d + HEAD_ROWS, k : k + 1]
                    add = add + x[d : d + HEAD_ROWS, :].astype(f32) * f
                if par:
                    to, row = r // t_ref.shape[1], r % t_ref.shape[1]
                    t_ref[to, row : row + HEAD_ROWS, at : at + wide] = add.astype(bf16)
                else:
                    total[r : r + HEAD_ROWS, at : at + wide] = add
                at += wide

    share = t_ref.shape[1]
    for to in range(t_ref.shape[0]):
        for n in range(key_ref.shape[0] // share):
            at = NSEL * BLK + n * ID
            t_ref[to, :, at : at + ID] = key_ref[n * share : (n + 1) * share]

    @pl.when(g == 1)
    def _():
        for group in range(2):
            for par in range(2):
                out_copy(group, par).wait()


def rest_stage(q, src, pieces, bias, own, rem_key, positions):
    heads = q.shape[1] // QK
    tall = heads // 2 * GROUP
    keys = bias.shape[2]
    every = NSEL * BLK
    share = q.shape[0] // positions
    wide = every + rem_key.shape[1] // share * ID
    return pl.pallas_call(
        functools.partial(rest_kernel, len(pieces)),
        out_shape=(
            jax.ShapeDtypeStruct((2, 2, tall, keys), bf16),
            jax.ShapeDtypeStruct((2, 2 * heads, GROUP), f32),
            jax.ShapeDtypeStruct((2, keys, LAT), bf16),
            jax.ShapeDtypeStruct((positions, share, wide), bf16),
        ),
        grid=(2,),
        in_specs=[smem(), rows_spec(q.shape[1])]
        + [vmem() for x in pieces]
        + [group_spec(1, keys), group_spec(2, tall, OWN), group_spec(2 * heads, GROUP)]
        + [group_spec(*rem_key.shape[1:])],
        out_specs=(
            anywhere(),
            group_spec(2 * heads, GROUP),
            group_spec(keys, LAT),
            pl.BlockSpec((positions // 2, share, wide), lambda g: (g, 0, 0)),
        ),
        scratch_shapes=[
            pltpu.VMEM((keys, KW), bf16),
            pltpu.VMEM((keys, KW), bf16),
            pltpu.VMEM((2, 2, tall, keys), bf16),
            pltpu.VMEM((GROUP, every), f32),
            pltpu.VMEM((tall, GROUP), f32),
            pltpu.SemaphoreType.DMA((4,)),
        ],
        compiler_params=params(1),
    )(src, far(q), *pieces, bias, far(own[0]), own[1], rem_key)


def context_kernel(f_ref, po_ref, pr_ref, vo_ref, vr_ref, ctx_ref):
    par = pl.program_id(1)
    n = f_ref.shape[0] // 4
    fs = [column(f_ref[pl.ds(pl.multiple_of((2 * k + par) * n, n), n), :]) for k in range(2)]
    out = nn(po_ref[...], vo_ref[...]) * fs[0] + nn(pr_ref[...], vr_ref[...]) * fs[1]
    out = out.astype(bf16)
    for k in range(n):
        at = pl.multiple_of((2 * k + par) * LAT, LAT)
        ctx_ref[:, pl.ds(at, LAT)] = out[k * GROUP : (k + 1) * GROUP]


def contexts(f, po, pr, vo, vr):
    heads = f.shape[1] // 2
    part = lambda x: pl.BlockSpec((None, None, *x.shape[2:]), lambda g, par: (g, par, 0, 0))
    group = lambda x: pl.BlockSpec((None, *x.shape[1:]), lambda g, par: (g, 0, 0))
    return pl.pallas_call(
        context_kernel,
        out_shape=jax.ShapeDtypeStruct((2 * GROUP, heads * LAT), bf16),
        grid=(2, 2),
        in_specs=[group(f), part(po), part(pr), group(vo), group(vr)],
        out_specs=pl.BlockSpec((GROUP, heads * LAT), lambda g, par: (g, 0)),
        compiler_params=params(2),
    )(f, far(po), far(pr), vo, vr)


JB = 8


def index_part(iq, keys, b):
    cols = [iq[:, (b * JB + n) * ID : (b * JB + n + 1) * ID] for n in range(JB)]
    return nt(jnp.concatenate(cols, 0), keys)


def index_kernel(h_ref, iq_ref, w_ref, own_ref, part_ref, bias_own, bias_rem, loss_ref, grad_ref, keys, acts):
    rows = iq_ref.shape[0]
    every = keys.shape[0]
    keys[:OWN] = own_ref[...]
    places = part_ref.shape[0]
    each = (every - OWN) // places
    for d in range(places):
        for n in range(each // rows):
            at = OWN + d * each + n * rows
            keys[at : at + rows] = part_ref[d, :, every + n * ID : every + (n + 1) * ID]
    sum_ = jnp.zeros((rows, every), f32)
    for b in range(IH // JB):
        act = index_part(iq_ref, keys[...], b)
        acts[b] = act.astype(bf16)
        for n in range(JB):
            j = b * JB + n
            sum_ = sum_ + jnp.maximum(act[n * rows : (n + 1) * rows], 0.0) * w_ref[:, j : j + 1]
    logits = sum_ * INDEX_SCALE
    logits = jnp.concatenate(
        [logits[:, :OWN] + bias_own[...], logits[:, OWN:] + bias_rem[...]], 1
    )
    top = jnp.max(logits, -1, keepdims=True)
    shifted = logits - top
    log_q = shifted - jnp.log(jnp.sum(jnp.exp(shifted), -1, keepdims=True))
    target = part_ref[0, :, :every].astype(f32)
    for n in range(1, places):
        target = target + part_ref[n, :, :every].astype(f32)
    target = target / H
    shown = log_q > 0.5 * NEG
    prob_q = jnp.where(shown, jnp.exp(log_q), 0.0)
    live = shown & (target > 0)
    safe = jnp.where(live, target, 1.0)
    terms = jnp.where(live, target * (jnp.log(safe) - log_q), 0.0)
    loss = jnp.sum(terms, -1, keepdims=True)
    eye = lax.broadcasted_iota(i32, (rows, rows), 0) == lax.broadcasted_iota(i32, (rows, rows), 1)
    loss_ref[...] = jnp.sum(jnp.where(eye, loss, 0.0), 0, keepdims=True)
    diff = prob_q - target
    for b in range(IH // JB):
        coef = []
        for n in range(JB):
            j = b * JB + n
            value = diff * (w_ref[:, j : j + 1] * INDEX_SCALE)
            seen = acts[b, n * rows : (n + 1) * rows].astype(f32) > 0
            coef.append(jnp.where(seen, value, 0.0).astype(bf16))
        got = nn(jnp.concatenate(coef, 0), keys[...])
        for n in range(JB):
            j = b * JB + n
            grad_ref[:, j * ID : (j + 1) * ID] = got[n * rows : (n + 1) * rows]


def index(h, iq, w, own, parts, bias_own, bias_rem):
    rows = iq.shape[0]
    heads = parts.shape[0]
    keys = NSEL * BLK
    group = lambda c, h: (h[0] // (heads // 2), 0, 0)
    flat = lambda c, h: (0, 0)
    return pl.pallas_call(
        index_kernel,
        out_shape=(
            jax.ShapeDtypeStruct((1, rows), f32),
            jax.ShapeDtypeStruct((rows, IH * ID), f32),
        ),
        grid_spec=pltpu.PrefetchScalarGridSpec(
            num_scalar_prefetch=1,
            grid=(1,),
            in_specs=[
                pl.BlockSpec((rows, IH * ID), flat),
                pl.BlockSpec((rows, IH), flat),
                pl.BlockSpec((None, OWN, ID), group),
                pl.BlockSpec(parts.shape, lambda c, h: (0, 0, 0)),
                pl.BlockSpec((None, rows, OWN), lambda c, h: (h[0], 0, 0)),
                pl.BlockSpec((None, 1, keys - OWN), group),
            ],
            out_specs=(pl.BlockSpec((1, rows), flat), pl.BlockSpec((rows, IH * ID), flat)),
            scratch_shapes=[
                pltpu.VMEM((keys, ID), bf16),
                pltpu.VMEM((IH // JB, JB * rows, keys), bf16),
            ],
        ),
        compiler_params=params(),
    )(h, iq, w, own, near(parts), bias_own, bias_rem)


def gather_head(x, heads):
    ring = [x]
    for d in (2, heads - 2, 4):
        ring.append(lax.ppermute(x, "head", [(i, (i + d) % heads) for i in range(heads)]))
    other = [lax.ppermute(r, "head", [(i, i ^ 1) for i in range(heads)]) for r in ring]
    return ring + other


def after(x, *first):
    return lax.optimization_barrier((x, *first))[0]


def swap(x, axis):
    return lax.all_to_all(x, axis, split_axis=0, concat_axis=0, tiled=True)


def body(query, latent, index_keys, index_query, index_weight, block_list, list_len, start):
    seqs = lax.axis_size("seq")
    heads = lax.axis_size("head")
    me = lax.axis_index("seq")
    h = lax.axis_index("head")
    h1 = h.astype(i32).reshape(1)
    blk_dev = latent.shape[0]
    request, place, own_idx = plan(
        me.astype(i32).reshape(1), block_list, list_len, seqs, blk_dev
    )
    asked = swap(request, "seq")
    out_l = send(h1, asked, latent, heads, 0, 1)
    in_l = swap(out_l, "seq")
    out_k = send(h1, after(asked, out_l), index_keys, heads, 0, 1)
    own_lat, own_key = own_rows(after(own_idx, out_k), latent, index_keys)
    own_key = own_key.reshape(2, OWN, ID)

    col = jnp.arange(OWN, dtype=i32)
    token = (col % (OWN // 2)) // CAPC * 2 + col // (OWN // 2)
    blocks = jnp.tile(own_idx.reshape(2, CAPC), (1, OWN // CAPC)) + me * blk_dev
    key_pos = blocks * BLK + token[None, :]
    row_pos = start[:, None] + jnp.arange(GROUP, dtype=i32)[None, :]
    bias_own = jnp.where(key_pos[:, None, :] <= row_pos[:, :, None], 0.0, NEG).astype(f32)
    used = jnp.where(place.reshape(2, REM) >= 0, 0.0, NEG).astype(f32)
    bias_rem = jnp.tile(used, (1, BLK // PARTS))[:, None, :]

    own = own_stage(query, own_lat, bias_own)
    back = jnp.array([0, 2, heads - 2, 4], i32)
    src = jnp.concatenate([h - back + heads, (h ^ 1) - back + heads]) % heads
    in_l, bias_rem, src, _ = lax.optimization_barrier((in_l, bias_rem, src, own[0]))
    packed = pack_lat(place, in_l)
    pieces = gather_head(packed, heads)
    in_k = swap(after(out_k, packed), "seq")
    packed_k = pack_key(place, in_k)
    p_r, factors, v_r, partial = rest_stage(
        query, src, pieces, bias_rem, own, packed_k, heads
    )
    parts = swap(partial, "head")
    context = contexts(after(factors, partial), own[0], p_r, own[2], v_r)
    share = index_query.shape[0]
    loss, grad = index(
        h1, index_query, index_weight, own_key, after(parts, context),
        bias_own.reshape(heads, share, OWN), bias_rem,
    )
    return context, loss.reshape(-1), grad


def solution(mesh):
    placed = (
        P("seq", "head"),
        P("seq", None),
        P("seq", None),
        P(("seq", "head"), None),
        P(("seq", "head"), None),
        P("seq", None),
        P("seq"),
        P("seq"),
    )
    return jax.shard_map(
        body,
        mesh=mesh,
        in_specs=placed,
        out_specs=(P("seq", "head"), P(("seq", "head")), P(("seq", "head"), None)),
        check_vma=False,
    )
```

```python
import functools
import math

import jax
import jax.numpy as jnp
from jax import lax
from jax.experimental import pallas as pl
from jax.experimental.pallas import tpu as pltpu
from jax.sharding import PartitionSpec as P

H = 128
LAT = 512
IH = 64
ID = 128
BLK = 64
NSEL = 32
GROUP = 128
CAPC = 8
QK = 576

PAIR = 2 * QK
KW = 640
SCALE = 192.0 ** -0.5
INDEX_SCALE = 128.0 ** -0.5
LOG2E = math.log2(math.e)
NEG = -1e30
OWN = CAPC * BLK
PARTS = 1
REM = NSEL - CAPC
VMEM_LIMIT = 56 * 1024 * 1024

f32 = jnp.float32
bf16 = jnp.bfloat16
i32 = jnp.int32


def params(n=1):
    return pltpu.CompilerParams(
        vmem_limit_bytes=VMEM_LIMIT, dimension_semantics=("arbitrary",) * n
    )


def smem():
    return pl.BlockSpec(memory_space=pltpu.SMEM)


def vmem():
    return pl.BlockSpec(memory_space=pltpu.VMEM)


def far(x):
    return pltpu.with_memory_space_constraint(x, pltpu.HBM)


def near(x):
    return pltpu.with_memory_space_constraint(x, pltpu.VMEM)


def nt(a, b):
    return lax.dot_general(a, b, (((1,), (1,)), ((), ())), preferred_element_type=f32)


def nn(a, b):
    return jnp.dot(a, b, preferred_element_type=f32)


def plan_kernel(seqs, blk_dev, me_ref, list_ref, len_ref, req_ref, place_ref, own_ref, count):
    cap = 2 * CAPC
    me = me_ref[0]
    req_ref[...] = jnp.full(req_ref.shape, -1, i32)
    for o in range(seqs):
        count[o] = 0
    for n in range(2 * REM):
        place_ref[n] = -1
    for n in range(2 * CAPC):
        own_ref[n] = -1
    for g in range(2):

        def entry(k, carry):
            own_n, rem_n = carry
            block = list_ref[g, k]
            owner = block // blk_dev
            local = block - owner * blk_dev
            mine = owner == me

            @pl.when(mine)
            def _():
                own_ref[g * CAPC + jnp.minimum(own_n, CAPC - 1)] = local

            @pl.when(jnp.logical_not(mine))
            def _():
                rank = jnp.minimum(count[owner], cap - 1)
                count[owner] = rank + 1
                at = owner * cap + rank
                req_ref[pl.ds(at, 1), :] = jnp.full((1, req_ref.shape[1]), local, i32)
                place_ref[g * REM + jnp.minimum(rem_n, REM - 1)] = at

            step = mine.astype(i32)
            return own_n + step, rem_n + 1 - step

        lax.fori_loop(0, len_ref[g], entry, (jnp.int32(0), jnp.int32(0)))


def plan(me, lists, lens, seqs, blk_dev):
    return pl.pallas_call(
        functools.partial(plan_kernel, seqs, blk_dev),
        out_shape=(
            jax.ShapeDtypeStruct((seqs * 2 * CAPC, blk_dev), i32),
            jax.ShapeDtypeStruct((2 * REM,), i32),
            jax.ShapeDtypeStruct((2 * CAPC,), i32),
        ),
        in_specs=[smem()] * 3,
        out_specs=(vmem(), smem(), smem()),
        scratch_shapes=[pltpu.SMEM((seqs,), i32)],
    )(me, lists, lens)


def send_kernel(h_ref, asked_ref, x_ref, out_ref):
    lane = lax.broadcasted_iota(i32, asked_ref.shape, 1)
    pick = (asked_ref[...] == lane).astype(f32).astype(bf16)
    out_ref[...] = nn(pick, x_ref[...]).astype(bf16)


def send(h, asked, x, heads, part, parts):
    rows, blocks = asked.shape
    width = x.shape[1] // heads // parts
    return pl.pallas_call(
        send_kernel,
        out_shape=jax.ShapeDtypeStruct((rows, width), bf16),
        grid_spec=pltpu.PrefetchScalarGridSpec(
            num_scalar_prefetch=1,
            grid=(1,),
            in_specs=[
                pl.BlockSpec((rows, blocks), lambda c, h: (0, 0)),
                pl.BlockSpec((blocks, width), lambda c, h: (0, h[0] * parts + part)),
            ],
            out_specs=pl.BlockSpec((rows, width), lambda c, h: (0, 0)),
        ),
        compiler_params=params(),
    )(h, near(asked), far(x))


def picker(idx_ref, rows, width):
    row = lax.broadcasted_iota(i32, (rows, width), 0)
    lane = lax.broadcasted_iota(i32, (rows, width), 1)
    want = jnp.full((rows, width), -1, i32)
    for r in range(rows):
        want = jnp.where(row == r, idx_ref[r], want)
    return (want == lane).astype(f32).astype(bf16)


def own_kernel(idx_ref, lat_ref, key_ref, lat_out, key_out):
    pick = picker(idx_ref, 2 * CAPC, lat_ref.shape[0])
    pairs = lat_ref.shape[1] // PAIR
    got = [nn(pick, lat_ref[:, i * PAIR : (i + 1) * PAIR]) for i in range(pairs)]
    for g in range(2):
        part = [x[g * CAPC : (g + 1) * CAPC] for x in got]
        lat_out[g] = jnp.concatenate(part, 0).astype(bf16)
    got = [nn(pick, key_ref[:, t * ID : (t + 1) * ID]) for t in range(2 * pairs)]
    for g in range(2):
        for par in range(2):
            part = [x[g * CAPC : (g + 1) * CAPC] for x in got[par::2]]
            key_out[g, par] = jnp.concatenate(part, 0).astype(bf16)


def own_rows(idx, latent, keys):
    blocks = latent.shape[0]
    steps = 8
    pairs = BLK // 2 // steps
    rows = pairs * CAPC
    return pl.pallas_call(
        own_kernel,
        out_shape=(
            jax.ShapeDtypeStruct((2, OWN // 2, PAIR), bf16),
            jax.ShapeDtypeStruct((2, 2, OWN // 2, ID), bf16),
        ),
        grid=(steps,),
        in_specs=[
            smem(),
            pl.BlockSpec((blocks, pairs * PAIR), lambda c: (0, c)),
            pl.BlockSpec((blocks, 2 * pairs * ID), lambda c: (0, c)),
        ],
        out_specs=(
            pl.BlockSpec((2, rows, PAIR), lambda c: (0, c, 0)),
            pl.BlockSpec((2, 2, rows, ID), lambda c: (0, 0, c, 0)),
        ),
        compiler_params=params(),
    )(idx, far(latent), far(keys))


def pack_lat_kernel(idx_ref, lat_ref, lat_out):
    pick = picker(idx_ref, 2 * REM, lat_ref.shape[0])
    pairs = lat_ref.shape[1] // PAIR
    got = [nn(pick, lat_ref[:, i * PAIR : (i + 1) * PAIR]) for i in range(pairs)]
    for g in range(2):
        part = [x[g * REM : (g + 1) * REM] for x in got]
        lat_out[g] = jnp.concatenate(part, 0).astype(bf16)


def pack_lat(idx, lat):
    pairs = lat.shape[1] // PAIR
    return pl.pallas_call(
        pack_lat_kernel,
        out_shape=jax.ShapeDtypeStruct((2, pairs * REM, PAIR), bf16),
        in_specs=[smem(), vmem()],
        out_specs=vmem(),
        compiler_params=params(0),
    )(idx, near(lat))


def part_pairs(tokens, c):
    pairs = tokens // 2 // PARTS
    return range(c * pairs, (c + 1) * pairs)


def pack_key_kernel(idx_ref, key_ref, key_out):
    pick = picker(idx_ref, 2 * REM, key_ref.shape[0])
    tokens = key_ref.shape[1] // ID
    got = [nn(pick, key_ref[:, t * ID : (t + 1) * ID]) for t in range(tokens)]
    for g in range(2):
        order = [2 * i + par for c in range(PARTS) for par in range(2) for i in part_pairs(tokens, c)]
        part = [got[t][g * REM : (g + 1) * REM] for t in order]
        rows = jnp.concatenate(part, 0).astype(bf16)
        key_out[g] = rows


def pack_key(idx, keys):
    tokens = keys.shape[1] // ID
    return pl.pallas_call(
        pack_key_kernel,
        out_shape=jax.ShapeDtypeStruct((2, tokens * REM, ID), bf16),
        in_specs=[smem(), vmem()],
        out_specs=vmem(),
        compiler_params=params(0),
    )(idx, near(keys))


def place_keys(x, ka, kb, at, rows):
    xf = x.astype(f32)
    lane = lax.broadcasted_iota(i32, (rows, KW), 1)
    gap = KW - QK
    even = jnp.where(lane < QK, xf[:, :KW], 0.0)
    odd = jnp.where(lane >= gap, xf[:, PAIR - KW :], 0.0)
    ka[pl.ds(at, rows), :] = even.astype(bf16)
    kb[pl.ds(at, rows), :] = pltpu.roll(even, gap, 1).astype(bf16)
    kb[pl.ds(at + rows, rows), :] = odd.astype(bf16)
    ka[pl.ds(at + rows, rows), :] = pltpu.roll(odd, QK, 1).astype(bf16)


def head_rows(q, par):
    first = range(par * (PAIR - KW), q.shape[1], PAIR)
    return jnp.concatenate([q[:, c : c + KW] for c in first], 0)


def score(rows, keys, bias):
    s = nt(rows, keys)
    if bias.shape[0] > 1:
        s = (s.reshape(-1, *bias.shape) + bias).reshape(s.shape)
    else:
        s = s + bias
    top = jnp.max(s, -1, keepdims=True)
    w = jnp.exp2((s - top) * (SCALE * LOG2E))
    return w, top, jnp.sum(w, -1, keepdims=True)


def lane_rows(x):
    eye = lax.broadcasted_iota(i32, (GROUP, GROUP), 0) == lax.broadcasted_iota(i32, (GROUP, GROUP), 1)
    parts = [x[r : r + GROUP] for r in range(0, x.shape[0], GROUP)]
    return jnp.concatenate(
        [jnp.sum(jnp.where(eye, part, 0.0), 0, keepdims=True) for part in parts], 0
    )


def column(rows):
    eye = lax.broadcasted_iota(i32, (GROUP, GROUP), 0) == lax.broadcasted_iota(i32, (GROUP, GROUP), 1)
    parts = [rows[n : n + 1] for n in range(rows.shape[0])]
    return jnp.concatenate(
        [jnp.sum(jnp.where(eye, part, 0.0), 1, keepdims=True) for part in parts], 0
    )


SOME = 2
HEAD_ROWS = 16


def own_stage_kernel(q_ref, own_ref, bias_ref, p_ref, st_ref, v_ref, ka, kb):
    place_keys(own_ref[...], ka, kb, 0, own_ref.shape[0])
    v_ref[...] = ka[:, :LAT]
    q, bias = q_ref[...], bias_ref[...]
    n = st_ref.shape[0] // 4
    for par, keys in ((0, ka), (1, kb)):
        w, top, sum_ = score(head_rows(q, par), keys[...], bias)
        p_ref[par] = w.astype(bf16)
        st_ref[par * n : (par + 1) * n] = lane_rows(top)
        st_ref[(par + 2) * n : (par + 3) * n] = lane_rows(sum_)


def anywhere():
    return pl.BlockSpec(memory_space=pl.ANY)


def group_spec(*shape):
    return pl.BlockSpec((None, *shape), lambda g: (g, *[0] * len(shape)))


def rows_spec(width):
    return pl.BlockSpec((GROUP, width), lambda g: (g, 0))


def own_stage(q, own, bias):
    heads = q.shape[1] // QK
    tall = heads // 2 * GROUP
    return pl.pallas_call(
        own_stage_kernel,
        out_shape=(
            jax.ShapeDtypeStruct((2, 2, tall, OWN), bf16),
            jax.ShapeDtypeStruct((2, 2 * heads, GROUP), f32),
            jax.ShapeDtypeStruct((2, OWN, LAT), bf16),
        ),
        grid=(2,),
        in_specs=[rows_spec(q.shape[1]), group_spec(*own.shape[1:]), group_spec(GROUP, OWN)],
        out_specs=(
            group_spec(2, tall, OWN),
            group_spec(2 * heads, GROUP),
            group_spec(OWN, LAT),
        ),
        scratch_shapes=[pltpu.VMEM((OWN, KW), bf16)] * 2,
        compiler_params=params(1),
    )(far(q), own, bias)


def rest_kernel(n, *refs):
    src_ref, q_ref, pieces, refs = refs[0], refs[1], refs[2 : 2 + n], refs[2 + n :]
    bias_ref, po_ref, st_ref, key_ref, p_ref, f_ref, v_ref, t_ref = refs[:8]
    ka, kb, ps, total, factors, sem = refs[8:]
    g = pl.program_id(0)
    for k, piece in enumerate(pieces):
        rows = piece.shape[1]
        at = pl.multiple_of(src_ref[k] * (2 * rows), 2 * rows)
        place_keys(piece[g], ka, kb, at, rows)
    v_ref[...] = ka[:, :LAT]
    q, bias = q_ref[...], bias_ref[...]
    n = st_ref.shape[0] // 4
    tall = n * GROUP
    c = SCALE * LOG2E

    def out_copy(group, par):
        return pltpu.make_async_copy(
            ps.at[group, par], p_ref.at[group, par], sem.at[group * 2 + par]
        )

    some = SOME * GROUP
    def head_sums(par):
        for r in range(0, GROUP, HEAD_ROWS):
            to, row = r // t_ref.shape[1], r % t_ref.shape[1]
            at = 0
            for k, x in enumerate((po_ref.at[par], ps.at[g, par])):
                wide = x.shape[1]
                add = total[r : r + HEAD_ROWS, at : at + wide] if par else 0.0
                for d in range(r, tall, GROUP):
                    f = factors[par, d : d + HEAD_ROWS, k : k + 1]
                    add = add + x[d : d + HEAD_ROWS, :].astype(f32) * f
                if par:
                    t_ref[to, row : row + HEAD_ROWS, at : at + wide] = add.astype(bf16)
                else:
                    total[r : r + HEAD_ROWS, at : at + wide] = add
                at += wide

    for par, keys in ((0, ka), (1, kb)):
        rows = head_rows(q, par)
        for i in range(0, n, SOME):
            here = slice(i * GROUP, i * GROUP + some)
            w, top, sum_ = score(rows[here], keys[...], bias)
            ps[g, par, here] = w.astype(bf16)
            top_o = column(st_ref[par * n + i : par * n + i + SOME])
            sum_o = column(st_ref[(par + 2) * n + i : (par + 2) * n + i + SOME])
            most = jnp.maximum(top_o, top)
            fs = [jnp.exp2((x - most) * c) for x in (top_o, top)]
            inv = 1.0 / (fs[0] * sum_o + fs[1] * sum_)
            for k in range(2):
                f = fs[k] * inv
                factors[par, here, k : k + 1] = f
                at = (2 * k + par) * n + i
                f_ref[at : at + SOME] = lane_rows(f)
        out_copy(g, par).start()
        head_sums(par)

    share = t_ref.shape[1]
    for to in range(t_ref.shape[0]):
        for n in range(key_ref.shape[0] // share):
            at = NSEL * BLK + n * ID
            t_ref[to, :, at : at + ID] = key_ref[n * share : (n + 1) * share]

    @pl.when(g == 1)
    def _():
        for group in range(2):
            for par in range(2):
                out_copy(group, par).wait()


def rest_stage(q, src, pieces, bias, own, rem_key, positions):
    heads = q.shape[1] // QK
    tall = heads // 2 * GROUP
    keys = bias.shape[2]
    every = NSEL * BLK
    share = q.shape[0] // positions
    wide = every + rem_key.shape[1] // share * ID
    return pl.pallas_call(
        functools.partial(rest_kernel, len(pieces)),
        out_shape=(
            jax.ShapeDtypeStruct((2, 2, tall, keys), bf16),
            jax.ShapeDtypeStruct((2, 2 * heads, GROUP), f32),
            jax.ShapeDtypeStruct((2, keys, LAT), bf16),
            jax.ShapeDtypeStruct((positions, share, wide), bf16),
        ),
        grid=(2,),
        in_specs=[smem(), rows_spec(q.shape[1])]
        + [vmem() for x in pieces]
        + [group_spec(1, keys), group_spec(2, tall, OWN), group_spec(2 * heads, GROUP)]
        + [group_spec(*rem_key.shape[1:])],
        out_specs=(
            anywhere(),
            group_spec(2 * heads, GROUP),
            group_spec(keys, LAT),
            pl.BlockSpec((positions // 2, share, wide), lambda g: (g, 0, 0)),
        ),
        scratch_shapes=[
            pltpu.VMEM((keys, KW), bf16),
            pltpu.VMEM((keys, KW), bf16),
            pltpu.VMEM((2, 2, tall, keys), bf16),
            pltpu.VMEM((GROUP, every), f32),
            pltpu.VMEM((2, tall, GROUP), f32),
            pltpu.SemaphoreType.DMA((4,)),
        ],
        compiler_params=params(1),
    )(src, far(q), *pieces, bias, far(own[0]), own[1], rem_key)


def context_kernel(f_ref, po_ref, pr_ref, vo_ref, vr_ref, ctx_ref):
    par = pl.program_id(1)
    n = f_ref.shape[0] // 4
    fs = [column(f_ref[pl.ds(pl.multiple_of((2 * k + par) * n, n), n), :]) for k in range(2)]
    out = nn(po_ref[...], vo_ref[...]) * fs[0] + nn(pr_ref[...], vr_ref[...]) * fs[1]
    out = out.astype(bf16)
    for k in range(n):
        at = pl.multiple_of((2 * k + par) * LAT, LAT)
        ctx_ref[:, pl.ds(at, LAT)] = out[k * GROUP : (k + 1) * GROUP]


def contexts(f, po, pr, vo, vr):
    heads = f.shape[1] // 2
    part = lambda x: pl.BlockSpec((None, None, *x.shape[2:]), lambda g, par: (g, par, 0, 0))
    group = lambda x: pl.BlockSpec((None, *x.shape[1:]), lambda g, par: (g, 0, 0))
    return pl.pallas_call(
        context_kernel,
        out_shape=jax.ShapeDtypeStruct((2 * GROUP, heads * LAT), bf16),
        grid=(2, 2),
        in_specs=[group(f), part(po), part(pr), group(vo), group(vr)],
        out_specs=pl.BlockSpec((GROUP, heads * LAT), lambda g, par: (g, 0)),
        compiler_params=params(2),
    )(f, far(po), far(pr), vo, vr)


JB = 8


def index_part(iq, keys, b):
    cols = [iq[:, (b * JB + n) * ID : (b * JB + n + 1) * ID] for n in range(JB)]
    return nt(jnp.concatenate(cols, 0), keys)


def index_kernel(h_ref, iq_ref, w_ref, own_ref, part_ref, bias_own, bias_rem, loss_ref, grad_ref, keys, acts):
    rows = iq_ref.shape[0]
    every = keys.shape[0]
    keys[:OWN] = own_ref[...]
    places = part_ref.shape[0]
    each = (every - OWN) // places
    for d in range(places):
        for n in range(each // rows):
            at = OWN + d * each + n * rows
            keys[at : at + rows] = part_ref[d, :, every + n * ID : every + (n + 1) * ID]
    sum_ = jnp.zeros((rows, every), f32)
    for b in range(IH // JB):
        act = index_part(iq_ref, keys[...], b)
        acts[b] = act.astype(bf16)
        for n in range(JB):
            j = b * JB + n
            sum_ = sum_ + jnp.maximum(act[n * rows : (n + 1) * rows], 0.0) * w_ref[:, j : j + 1]
    logits = sum_ * INDEX_SCALE
    logits = jnp.concatenate(
        [logits[:, :OWN] + bias_own[...], logits[:, OWN:] + bias_rem[...]], 1
    )
    top = jnp.max(logits, -1, keepdims=True)
    shifted = logits - top
    log_q = shifted - jnp.log(jnp.sum(jnp.exp(shifted), -1, keepdims=True))
    target = part_ref[0, :, :every].astype(f32)
    for n in range(1, places):
        target = target + part_ref[n, :, :every].astype(f32)
    target = target / H
    shown = log_q > 0.5 * NEG
    prob_q = jnp.where(shown, jnp.exp(log_q), 0.0)
    live = shown & (target > 0)
    safe = jnp.where(live, target, 1.0)
    terms = jnp.where(live, target * (jnp.log(safe) - log_q), 0.0)
    loss = jnp.sum(terms, -1, keepdims=True)
    eye = lax.broadcasted_iota(i32, (rows, rows), 0) == lax.broadcasted_iota(i32, (rows, rows), 1)
    loss_ref[...] = jnp.sum(jnp.where(eye, loss, 0.0), 0, keepdims=True)
    diff = prob_q - target
    for b in range(IH // JB):
        coef = []
        for n in range(JB):
            j = b * JB + n
            value = diff * (w_ref[:, j : j + 1] * INDEX_SCALE)
            seen = acts[b, n * rows : (n + 1) * rows].astype(f32) > 0
            coef.append(jnp.where(seen, value, 0.0).astype(bf16))
        got = nn(jnp.concatenate(coef, 0), keys[...])
        for n in range(JB):
            j = b * JB + n
            grad_ref[:, j * ID : (j + 1) * ID] = got[n * rows : (n + 1) * rows]


def index(h, iq, w, own, parts, bias_own, bias_rem):
    rows = iq.shape[0]
    heads = parts.shape[0]
    keys = NSEL * BLK
    group = lambda c, h: (h[0] // (heads // 2), 0, 0)
    flat = lambda c, h: (0, 0)
    return pl.pallas_call(
        index_kernel,
        out_shape=(
            jax.ShapeDtypeStruct((1, rows), f32),
            jax.ShapeDtypeStruct((rows, IH * ID), f32),
        ),
        grid_spec=pltpu.PrefetchScalarGridSpec(
            num_scalar_prefetch=1,
            grid=(1,),
            in_specs=[
                pl.BlockSpec((rows, IH * ID), flat),
                pl.BlockSpec((rows, IH), flat),
                pl.BlockSpec((None, OWN, ID), group),
                pl.BlockSpec(parts.shape, lambda c, h: (0, 0, 0)),
                pl.BlockSpec((None, rows, OWN), lambda c, h: (h[0], 0, 0)),
                pl.BlockSpec((None, 1, keys - OWN), group),
            ],
            out_specs=(pl.BlockSpec((1, rows), flat), pl.BlockSpec((rows, IH * ID), flat)),
            scratch_shapes=[
                pltpu.VMEM((keys, ID), bf16),
                pltpu.VMEM((IH // JB, JB * rows, keys), bf16),
            ],
        ),
        compiler_params=params(),
    )(h, iq, w, own, near(parts), bias_own, bias_rem)


def gather_head(x, heads):
    ring = [x]
    for d in (2, heads - 2, 4):
        ring.append(lax.ppermute(x, "head", [(i, (i + d) % heads) for i in range(heads)]))
    other = [lax.ppermute(r, "head", [(i, i ^ 1) for i in range(heads)]) for r in ring]
    return ring + other


def after(x, *first):
    return lax.optimization_barrier((x, *first))[0]


def swap(x, axis):
    return lax.all_to_all(x, axis, split_axis=0, concat_axis=0, tiled=True)


def body(query, latent, index_keys, index_query, index_weight, block_list, list_len, start):
    seqs = lax.axis_size("seq")
    heads = lax.axis_size("head")
    me = lax.axis_index("seq")
    h = lax.axis_index("head")
    h1 = h.astype(i32).reshape(1)
    blk_dev = latent.shape[0]
    request, place, own_idx = plan(
        me.astype(i32).reshape(1), block_list, list_len, seqs, blk_dev
    )
    asked = swap(request, "seq")
    out_l = send(h1, asked, latent, heads, 0, 1)
    in_l = swap(out_l, "seq")
    out_k = send(h1, after(asked, out_l), index_keys, heads, 0, 1)
    own_lat, own_key = own_rows(after(own_idx, out_k), latent, index_keys)
    own_key = own_key.reshape(2, OWN, ID)

    col = jnp.arange(OWN, dtype=i32)
    token = (col % (OWN // 2)) // CAPC * 2 + col // (OWN // 2)
    blocks = jnp.tile(own_idx.reshape(2, CAPC), (1, OWN // CAPC)) + me * blk_dev
    key_pos = blocks * BLK + token[None, :]
    row_pos = start[:, None] + jnp.arange(GROUP, dtype=i32)[None, :]
    bias_own = jnp.where(key_pos[:, None, :] <= row_pos[:, :, None], 0.0, NEG).astype(f32)
    used = jnp.where(place.reshape(2, REM) >= 0, 0.0, NEG).astype(f32)
    bias_rem = jnp.tile(used, (1, BLK // PARTS))[:, None, :]

    own = own_stage(query, own_lat, bias_own)
    back = jnp.array([0, 2, heads - 2, 4], i32)
    src = jnp.concatenate([h - back + heads, (h ^ 1) - back + heads]) % heads
    in_l, bias_rem, src, _ = lax.optimization_barrier((in_l, bias_rem, src, own[0]))
    packed = pack_lat(place, in_l)
    pieces = gather_head(packed, heads)
    in_k = swap(after(out_k, packed), "seq")
    packed_k = pack_key(place, in_k)
    p_r, factors, v_r, partial = rest_stage(
        query, src, pieces, bias_rem, own, packed_k, heads
    )
    parts = swap(partial, "head")
    context = contexts(after(factors, partial), own[0], p_r, own[2], v_r)
    share = index_query.shape[0]
    loss, grad = index(
        h1, index_query, index_weight, own_key, after(parts, context),
        bias_own.reshape(heads, share, OWN), bias_rem,
    )
    return context, loss.reshape(-1), grad


def solution(mesh):
    placed = (
        P("seq", "head"),
        P("seq", None),
        P("seq", None),
        P(("seq", "head"), None),
        P(("seq", "head"), None),
        P("seq", None),
        P("seq"),
        P("seq"),
    )
    return jax.shard_map(
        body,
        mesh=mesh,
        in_specs=placed,
        out_specs=(P("seq", "head"), P(("seq", "head")), P(("seq", "head"), None)),
        check_vma=False,
    )
```

```python
import functools
import math

import jax
import jax.numpy as jnp
from jax import lax
from jax.experimental import pallas as pl
from jax.experimental.pallas import tpu as pltpu
from jax.sharding import PartitionSpec as P

H = 128
LAT = 512
IH = 64
ID = 128
BLK = 64
NSEL = 32
GROUP = 128
CAPC = 8
QK = 576

PAIR = 2 * QK
KW = 640
SCALE = 192.0 ** -0.5
INDEX_SCALE = 128.0 ** -0.5
LOG2E = math.log2(math.e)
NEG = -1e30
OWN = CAPC * BLK
PARTS = 1
REM = NSEL - CAPC
VMEM_LIMIT = 56 * 1024 * 1024

f32 = jnp.float32
bf16 = jnp.bfloat16
i32 = jnp.int32


def params(n=1):
    return pltpu.CompilerParams(
        vmem_limit_bytes=VMEM_LIMIT, dimension_semantics=("arbitrary",) * n
    )


def smem():
    return pl.BlockSpec(memory_space=pltpu.SMEM)


def vmem():
    return pl.BlockSpec(memory_space=pltpu.VMEM)


def far(x):
    return pltpu.with_memory_space_constraint(x, pltpu.HBM)


def near(x):
    return pltpu.with_memory_space_constraint(x, pltpu.VMEM)


def nt(a, b):
    return lax.dot_general(a, b, (((1,), (1,)), ((), ())), preferred_element_type=f32)


def nn(a, b):
    return jnp.dot(a, b, preferred_element_type=f32)


def plan_kernel(seqs, blk_dev, me_ref, list_ref, len_ref, req_ref, place_ref, own_ref, count):
    cap = 2 * CAPC
    me = me_ref[0]
    req_ref[...] = jnp.full(req_ref.shape, -1, i32)
    for o in range(seqs):
        count[o] = 0
    for n in range(2 * REM):
        place_ref[n] = -1
    for n in range(2 * CAPC):
        own_ref[n] = -1
    for g in range(2):

        def entry(k, carry):
            own_n, rem_n = carry
            block = list_ref[g, k]
            owner = block // blk_dev
            local = block - owner * blk_dev
            mine = owner == me

            @pl.when(mine)
            def _():
                own_ref[g * CAPC + jnp.minimum(own_n, CAPC - 1)] = local

            @pl.when(jnp.logical_not(mine))
            def _():
                rank = jnp.minimum(count[owner], cap - 1)
                count[owner] = rank + 1
                at = owner * cap + rank
                req_ref[pl.ds(at, 1), :] = jnp.full((1, req_ref.shape[1]), local, i32)
                place_ref[g * REM + jnp.minimum(rem_n, REM - 1)] = at

            step = mine.astype(i32)
            return own_n + step, rem_n + 1 - step

        lax.fori_loop(0, len_ref[g], entry, (jnp.int32(0), jnp.int32(0)))


def plan(me, lists, lens, seqs, blk_dev):
    return pl.pallas_call(
        functools.partial(plan_kernel, seqs, blk_dev),
        out_shape=(
            jax.ShapeDtypeStruct((seqs * 2 * CAPC, blk_dev), i32),
            jax.ShapeDtypeStruct((2 * REM,), i32),
            jax.ShapeDtypeStruct((2 * CAPC,), i32),
        ),
        in_specs=[smem()] * 3,
        out_specs=(vmem(), smem(), smem()),
        scratch_shapes=[pltpu.SMEM((seqs,), i32)],
    )(me, lists, lens)


def send_kernel(h_ref, asked_ref, x_ref, out_ref):
    lane = lax.broadcasted_iota(i32, asked_ref.shape, 1)
    pick = (asked_ref[...] == lane).astype(f32).astype(bf16)
    out_ref[...] = nn(pick, x_ref[...]).astype(bf16)


def send(h, asked, x, heads, part, parts):
    rows, blocks = asked.shape
    steps = 2
    width = x.shape[1] // heads // parts // steps
    return pl.pallas_call(
        send_kernel,
        out_shape=jax.ShapeDtypeStruct((rows, width * steps), bf16),
        grid_spec=pltpu.PrefetchScalarGridSpec(
            num_scalar_prefetch=1,
            grid=(steps,),
            in_specs=[
                pl.BlockSpec((rows, blocks), lambda c, h: (0, 0)),
                pl.BlockSpec((blocks, width), lambda c, h: (0, (h[0] * parts + part) * steps + c)),
            ],
            out_specs=pl.BlockSpec((rows, width), lambda c, h: (0, c)),
        ),
        compiler_params=params(),
    )(h, near(asked), far(x))


def picker(idx_ref, rows, width):
    row = lax.broadcasted_iota(i32, (rows, width), 0)
    lane = lax.broadcasted_iota(i32, (rows, width), 1)
    want = jnp.full((rows, width), -1, i32)
    for r in range(rows):
        want = jnp.where(row == r, idx_ref[r], want)
    return (want == lane).astype(f32).astype(bf16)


def own_kernel(idx_ref, lat_ref, key_ref, lat_out, key_out):
    pick = picker(idx_ref, 2 * CAPC, lat_ref.shape[0])
    pairs = lat_ref.shape[1] // PAIR
    got = [nn(pick, lat_ref[:, i * PAIR : (i + 1) * PAIR]) for i in range(pairs)]
    for g in range(2):
        part = [x[g * CAPC : (g + 1) * CAPC] for x in got]
        lat_out[g] = jnp.concatenate(part, 0).astype(bf16)
    got = [nn(pick, key_ref[:, t * ID : (t + 1) * ID]) for t in range(2 * pairs)]
    for g in range(2):
        for par in range(2):
            part = [x[g * CAPC : (g + 1) * CAPC] for x in got[par::2]]
            key_out[g, par] = jnp.concatenate(part, 0).astype(bf16)


def own_rows(idx, latent, keys):
    blocks = latent.shape[0]
    steps = 8
    pairs = BLK // 2 // steps
    rows = pairs * CAPC
    return pl.pallas_call(
        own_kernel,
        out_shape=(
            jax.ShapeDtypeStruct((2, OWN // 2, PAIR), bf16),
            jax.ShapeDtypeStruct((2, 2, OWN // 2, ID), bf16),
        ),
        grid=(steps,),
        in_specs=[
            smem(),
            pl.BlockSpec((blocks, pairs * PAIR), lambda c: (0, c)),
            pl.BlockSpec((blocks, 2 * pairs * ID), lambda c: (0, c)),
        ],
        out_specs=(
            pl.BlockSpec((2, rows, PAIR), lambda c: (0, c, 0)),
            pl.BlockSpec((2, 2, rows, ID), lambda c: (0, 0, c, 0)),
        ),
        compiler_params=params(),
    )(idx, far(latent), far(keys))


def pack_lat_kernel(idx_ref, lat_ref, lat_out):
    pick = picker(idx_ref, 2 * REM, lat_ref.shape[0])
    pairs = lat_ref.shape[1] // PAIR
    got = [nn(pick, lat_ref[:, i * PAIR : (i + 1) * PAIR]) for i in range(pairs)]
    for g in range(2):
        part = [x[g * REM : (g + 1) * REM] for x in got]
        lat_out[g] = jnp.concatenate(part, 0).astype(bf16)


def pack_lat(idx, lat):
    pairs = lat.shape[1] // PAIR
    return pl.pallas_call(
        pack_lat_kernel,
        out_shape=jax.ShapeDtypeStruct((2, pairs * REM, PAIR), bf16),
        in_specs=[smem(), vmem()],
        out_specs=vmem(),
        compiler_params=params(0),
    )(idx, near(lat))


def part_pairs(tokens, c):
    pairs = tokens // 2 // PARTS
    return range(c * pairs, (c + 1) * pairs)


def pack_key_kernel(idx_ref, key_ref, key_out):
    pick = picker(idx_ref, 2 * REM, key_ref.shape[0])
    tokens = key_ref.shape[1] // ID
    got = [nn(pick, key_ref[:, t * ID : (t + 1) * ID]) for t in range(tokens)]
    for g in range(2):
        order = [2 * i + par for c in range(PARTS) for par in range(2) for i in part_pairs(tokens, c)]
        part = [got[t][g * REM : (g + 1) * REM] for t in order]
        rows = jnp.concatenate(part, 0).astype(bf16)
        key_out[g] = rows


def pack_key(idx, keys):
    tokens = keys.shape[1] // ID
    return pl.pallas_call(
        pack_key_kernel,
        out_shape=jax.ShapeDtypeStruct((2, tokens * REM, ID), bf16),
        in_specs=[smem(), vmem()],
        out_specs=vmem(),
        compiler_params=params(0),
    )(idx, near(keys))


def place_keys(x, ka, kb, at, rows):
    xf = x.astype(f32)
    lane = lax.broadcasted_iota(i32, (rows, KW), 1)
    gap = KW - QK
    even = jnp.where(lane < QK, xf[:, :KW], 0.0)
    odd = jnp.where(lane >= gap, xf[:, PAIR - KW :], 0.0)
    ka[pl.ds(at, rows), :] = even.astype(bf16)
    kb[pl.ds(at, rows), :] = pltpu.roll(even, gap, 1).astype(bf16)
    kb[pl.ds(at + rows, rows), :] = odd.astype(bf16)
    ka[pl.ds(at + rows, rows), :] = pltpu.roll(odd, QK, 1).astype(bf16)


def head_rows(q, par):
    first = range(par * (PAIR - KW), q.shape[1], PAIR)
    return jnp.concatenate([q[:, c : c + KW] for c in first], 0)


def score(rows, keys, bias):
    s = nt(rows, keys)
    if bias.shape[0] > 1:
        s = (s.reshape(-1, *bias.shape) + bias).reshape(s.shape)
    else:
        s = s + bias
    top = jnp.max(s, -1, keepdims=True)
    w = jnp.exp2((s - top) * (SCALE * LOG2E))
    return w, top, jnp.sum(w, -1, keepdims=True)


def lane_rows(x):
    eye = lax.broadcasted_iota(i32, (GROUP, GROUP), 0) == lax.broadcasted_iota(i32, (GROUP, GROUP), 1)
    parts = [x[r : r + GROUP] for r in range(0, x.shape[0], GROUP)]
    return jnp.concatenate(
        [jnp.sum(jnp.where(eye, part, 0.0), 0, keepdims=True) for part in parts], 0
    )


def column(rows):
    eye = lax.broadcasted_iota(i32, (GROUP, GROUP), 0) == lax.broadcasted_iota(i32, (GROUP, GROUP), 1)
    parts = [rows[n : n + 1] for n in range(rows.shape[0])]
    return jnp.concatenate(
        [jnp.sum(jnp.where(eye, part, 0.0), 1, keepdims=True) for part in parts], 0
    )


SOME = 2
HEAD_ROWS = 16


def own_stage_kernel(q_ref, own_ref, bias_ref, p_ref, st_ref, v_ref, ka, kb):
    place_keys(own_ref[...], ka, kb, 0, own_ref.shape[0])
    v_ref[...] = ka[:, :LAT]
    q, bias = q_ref[...], bias_ref[...]
    n = st_ref.shape[0] // 4
    for par, keys in ((0, ka), (1, kb)):
        w, top, sum_ = score(head_rows(q, par), keys[...], bias)
        p_ref[par] = w.astype(bf16)
        st_ref[par * n : (par + 1) * n] = lane_rows(top)
        st_ref[(par + 2) * n : (par + 3) * n] = lane_rows(sum_)


def anywhere():
    return pl.BlockSpec(memory_space=pl.ANY)


def group_spec(*shape):
    return pl.BlockSpec((None, *shape), lambda g: (g, *[0] * len(shape)))


def rows_spec(width):
    return pl.BlockSpec((GROUP, width), lambda g: (g, 0))


def own_stage(q, own, bias):
    heads = q.shape[1] // QK
    tall = heads // 2 * GROUP
    return pl.pallas_call(
        own_stage_kernel,
        out_shape=(
            jax.ShapeDtypeStruct((2, 2, tall, OWN), bf16),
            jax.ShapeDtypeStruct((2, 2 * heads, GROUP), f32),
            jax.ShapeDtypeStruct((2, OWN, LAT), bf16),
        ),
        grid=(2,),
        in_specs=[rows_spec(q.shape[1]), group_spec(*own.shape[1:]), group_spec(GROUP, OWN)],
        out_specs=(
            group_spec(2, tall, OWN),
            group_spec(2 * heads, GROUP),
            group_spec(OWN, LAT),
        ),
        scratch_shapes=[pltpu.VMEM((OWN, KW), bf16)] * 2,
        compiler_params=params(1),
    )(far(q), own, bias)


def rest_kernel(n, *refs):
    src_ref, q_ref, pieces, refs = refs[0], refs[1], refs[2 : 2 + n], refs[2 + n :]
    bias_ref, po_ref, st_ref, key_ref, p_ref, f_ref, v_ref, t_ref = refs[:8]
    ka, kb, ps, total, factors, sem = refs[8:]
    g = pl.program_id(0)
    for k, piece in enumerate(pieces):
        rows = piece.shape[1]
        at = pl.multiple_of(src_ref[k] * (2 * rows), 2 * rows)
        place_keys(piece[g], ka, kb, at, rows)
    v_ref[...] = ka[:, :LAT]
    q, bias = q_ref[...], bias_ref[0:1]
    n = st_ref.shape[0] // 4
    tall = n * GROUP
    c = SCALE * LOG2E

    def out_copy(group, par):
        return pltpu.make_async_copy(
            ps.at[group, par], p_ref.at[group, par], sem.at[group * 2 + par]
        )

    some = SOME * GROUP
    def head_sums(par):
        for r in range(0, GROUP, HEAD_ROWS):
            to, row = r // t_ref.shape[1], r % t_ref.shape[1]
            at = 0
            for k, x in enumerate((po_ref.at[par], ps.at[g, par])):
                wide = x.shape[1]
                add = total[r : r + HEAD_ROWS, at : at + wide] if par else 0.0
                for d in range(r, tall, GROUP):
                    f = factors[par, d : d + HEAD_ROWS, k : k + 1]
                    add = add + x[d : d + HEAD_ROWS, :].astype(f32) * f
                if par:
                    t_ref[to, row : row + HEAD_ROWS, at : at + wide] = add.astype(bf16)
                else:
                    total[r : r + HEAD_ROWS, at : at + wide] = add
                at += wide

    for par, keys in ((0, ka), (1, kb)):
        rows = head_rows(q, par)
        for i in range(0, n, SOME):
            here = slice(i * GROUP, i * GROUP + some)
            w, top, sum_ = score(rows[here], keys[...], bias)
            ps[g, par, here] = w.astype(bf16)
            top_o = column(st_ref[par * n + i : par * n + i + SOME])
            sum_o = column(st_ref[(par + 2) * n + i : (par + 2) * n + i + SOME])
            most = jnp.maximum(top_o, top)
            fs = [jnp.exp2((x - most) * c) for x in (top_o, top)]
            inv = 1.0 / (fs[0] * sum_o + fs[1] * sum_)
            for k in range(2):
                f = fs[k] * inv
                factors[par, here, k : k + 1] = f
                at = (2 * k + par) * n + i
                f_ref[at : at + SOME] = lane_rows(f)
        out_copy(g, par).start()
        head_sums(par)

    share = t_ref.shape[1]
    for to in range(t_ref.shape[0]):
        for n in range(key_ref.shape[0] // share):
            at = NSEL * BLK + n * ID
            t_ref[to, :, at : at + ID] = key_ref[n * share : (n + 1) * share]

    @pl.when(g == 1)
    def _():
        for group in range(2):
            for par in range(2):
                out_copy(group, par).wait()


def rest_stage(q, src, pieces, bias, own, rem_key, positions):
    heads = q.shape[1] // QK
    tall = heads // 2 * GROUP
    keys = bias.shape[2]
    every = NSEL * BLK
    share = q.shape[0] // positions
    wide = every + rem_key.shape[1] // share * ID
    return pl.pallas_call(
        functools.partial(rest_kernel, len(pieces)),
        out_shape=(
            jax.ShapeDtypeStruct((2, 2, tall, keys), bf16),
            jax.ShapeDtypeStruct((2, 2 * heads, GROUP), f32),
            jax.ShapeDtypeStruct((2, keys, LAT), bf16),
            jax.ShapeDtypeStruct((positions, share, wide), bf16),
        ),
        grid=(2,),
        in_specs=[smem(), rows_spec(q.shape[1])]
        + [vmem() for x in pieces]
        + [group_spec(8, keys), group_spec(2, tall, OWN), group_spec(2 * heads, GROUP)]
        + [group_spec(*rem_key.shape[1:])],
        out_specs=(
            anywhere(),
            group_spec(2 * heads, GROUP),
            group_spec(keys, LAT),
            pl.BlockSpec((positions // 2, share, wide), lambda g: (g, 0, 0)),
        ),
        scratch_shapes=[
            pltpu.VMEM((keys, KW), bf16),
            pltpu.VMEM((keys, KW), bf16),
            pltpu.VMEM((2, 2, tall, keys), bf16),
            pltpu.VMEM((GROUP, every), f32),
            pltpu.VMEM((2, tall, GROUP), f32),
            pltpu.SemaphoreType.DMA((4,)),
        ],
        compiler_params=params(1),
    )(src, far(q), *pieces, bias, far(own[0]), own[1], rem_key)


def context_kernel(f_ref, po_ref, pr_ref, vo_ref, vr_ref, ctx_ref):
    par = pl.program_id(1)
    n = f_ref.shape[0] // 4
    fs = [column(f_ref[pl.ds(pl.multiple_of((2 * k + par) * n, n), n), :]) for k in range(2)]
    out = nn(po_ref[...], vo_ref[...]) * fs[0] + nn(pr_ref[...], vr_ref[...]) * fs[1]
    out = out.astype(bf16)
    for k in range(n):
        at = pl.multiple_of((2 * k + par) * LAT, LAT)
        ctx_ref[:, pl.ds(at, LAT)] = out[k * GROUP : (k + 1) * GROUP]


def contexts(f, po, pr, vo, vr):
    heads = f.shape[1] // 2
    part = lambda x: pl.BlockSpec((None, None, *x.shape[2:]), lambda g, par: (g, par, 0, 0))
    group = lambda x: pl.BlockSpec((None, *x.shape[1:]), lambda g, par: (g, 0, 0))
    return pl.pallas_call(
        context_kernel,
        out_shape=jax.ShapeDtypeStruct((2 * GROUP, heads * LAT), bf16),
        grid=(2, 2),
        in_specs=[group(f), part(po), part(pr), group(vo), group(vr)],
        out_specs=pl.BlockSpec((GROUP, heads * LAT), lambda g, par: (g, 0)),
        compiler_params=params(2),
    )(f, far(po), far(pr), vo, vr)


JB = 8


def index_part(iq, keys, b):
    cols = [iq[:, (b * JB + n) * ID : (b * JB + n + 1) * ID] for n in range(JB)]
    return nt(jnp.concatenate(cols, 0), keys)


def index_kernel(h_ref, iq_ref, w_ref, own_ref, part_ref, bias_own, bias_rem, loss_ref, grad_ref, keys, acts):
    rows = iq_ref.shape[0]
    every = keys.shape[0]
    keys[:OWN] = own_ref[...]
    places = part_ref.shape[0]
    each = (every - OWN) // places
    for d in range(places):
        for n in range(each // rows):
            at = OWN + d * each + n * rows
            keys[at : at + rows] = part_ref[d, :, every + n * ID : every + (n + 1) * ID]
    sum_ = jnp.zeros((rows, every), f32)
    for b in range(IH // JB):
        act = index_part(iq_ref, keys[...], b)
        acts[b] = act.astype(bf16)
        for n in range(JB):
            j = b * JB + n
            sum_ = sum_ + jnp.maximum(act[n * rows : (n + 1) * rows], 0.0) * w_ref[:, j : j + 1]
    logits = sum_ * INDEX_SCALE
    logits = jnp.concatenate(
        [logits[:, :OWN] + bias_own[...], logits[:, OWN:] + bias_rem[0:1]], 1
    )
    top = jnp.max(logits, -1, keepdims=True)
    shifted = logits - top
    log_q = shifted - jnp.log(jnp.sum(jnp.exp(shifted), -1, keepdims=True))
    target = part_ref[0, :, :every].astype(f32)
    for n in range(1, places):
        target = target + part_ref[n, :, :every].astype(f32)
    target = target / H
    shown = log_q > 0.5 * NEG
    prob_q = jnp.where(shown, jnp.exp(log_q), 0.0)
    live = shown & (target > 0)
    safe = jnp.where(live, target, 1.0)
    terms = jnp.where(live, target * (jnp.log(safe) - log_q), 0.0)
    loss = jnp.sum(terms, -1, keepdims=True)
    eye = lax.broadcasted_iota(i32, (rows, rows), 0) == lax.broadcasted_iota(i32, (rows, rows), 1)
    loss_ref[...] = jnp.sum(jnp.where(eye, loss, 0.0), 0, keepdims=True)
    diff = prob_q - target
    for b in range(IH // JB):
        coef = []
        for n in range(JB):
            j = b * JB + n
            value = diff * (w_ref[:, j : j + 1] * INDEX_SCALE)
            seen = acts[b, n * rows : (n + 1) * rows].astype(f32) > 0
            coef.append(jnp.where(seen, value, 0.0).astype(bf16))
        got = nn(jnp.concatenate(coef, 0), keys[...])
        for n in range(JB):
            j = b * JB + n
            grad_ref[:, j * ID : (j + 1) * ID] = got[n * rows : (n + 1) * rows]


def index(h, iq, w, own, parts, bias_own, bias_rem):
    rows = iq.shape[0]
    heads = parts.shape[0]
    keys = NSEL * BLK
    group = lambda c, h: (h[0] // (heads // 2), 0, 0)
    flat = lambda c, h: (0, 0)
    return pl.pallas_call(
        index_kernel,
        out_shape=(
            jax.ShapeDtypeStruct((1, rows), f32),
            jax.ShapeDtypeStruct((rows, IH * ID), f32),
        ),
        grid_spec=pltpu.PrefetchScalarGridSpec(
            num_scalar_prefetch=1,
            grid=(1,),
            in_specs=[
                pl.BlockSpec((rows, IH * ID), flat),
                pl.BlockSpec((rows, IH), flat),
                pl.BlockSpec((None, OWN, ID), group),
                pl.BlockSpec(parts.shape, lambda c, h: (0, 0, 0)),
                pl.BlockSpec((None, rows, OWN), lambda c, h: (h[0], 0, 0)),
                pl.BlockSpec((None, 8, keys - OWN), group),
            ],
            out_specs=(pl.BlockSpec((1, rows), flat), pl.BlockSpec((rows, IH * ID), flat)),
            scratch_shapes=[
                pltpu.VMEM((keys, ID), bf16),
                pltpu.VMEM((IH // JB, JB * rows, keys), bf16),
            ],
        ),
        compiler_params=params(),
    )(h, iq, w, own, near(parts), bias_own, bias_rem)


def gather_head(x, heads):
    ring = [x]
    for d in (2, heads - 2, 4):
        ring.append(lax.ppermute(x, "head", [(i, (i + d) % heads) for i in range(heads)]))
    other = [lax.ppermute(r, "head", [(i, i ^ 1) for i in range(heads)]) for r in ring]
    return ring + other


def after(x, *first):
    return lax.optimization_barrier((x, *first))[0]


def swap(x, axis):
    return lax.all_to_all(x, axis, split_axis=0, concat_axis=0, tiled=True)


def body(query, latent, index_keys, index_query, index_weight, block_list, list_len, start):
    seqs = lax.axis_size("seq")
    heads = lax.axis_size("head")
    me = lax.axis_index("seq")
    h = lax.axis_index("head")
    h1 = h.astype(i32).reshape(1)
    blk_dev = latent.shape[0]
    request, place, own_idx = plan(
        me.astype(i32).reshape(1), block_list, list_len, seqs, blk_dev
    )
    asked = swap(request, "seq")
    out_l = send(h1, asked, latent, heads, 0, 1)
    in_l = swap(out_l, "seq")
    out_k = send(h1, after(asked, out_l), index_keys, heads, 0, 1)
    own_lat, own_key = own_rows(after(own_idx, out_k), latent, index_keys)
    own_key = own_key.reshape(2, OWN, ID)

    col = jnp.arange(OWN, dtype=i32)
    token = (col % (OWN // 2)) // CAPC * 2 + col // (OWN // 2)
    blocks = jnp.tile(own_idx.reshape(2, CAPC), (1, OWN // CAPC)) + me * blk_dev
    key_pos = blocks * BLK + token[None, :]
    row_pos = start[:, None] + jnp.arange(GROUP, dtype=i32)[None, :]
    bias_own = jnp.where(key_pos[:, None, :] <= row_pos[:, :, None], 0.0, NEG).astype(f32)
    used = jnp.where(place.reshape(2, REM) >= 0, 0.0, NEG).astype(f32)
    bias_rem = jnp.tile(used, (1, BLK // PARTS))
    bias_rem = jnp.broadcast_to(bias_rem[:, None, :], (2, 8, bias_rem.shape[1]))

    own = own_stage(query, own_lat, bias_own)
    back = jnp.array([0, 2, heads - 2, 4], i32)
    src = jnp.concatenate([h - back + heads, (h ^ 1) - back + heads]) % heads
    in_l, bias_rem, src, _ = lax.optimization_barrier((in_l, bias_rem, src, own[0]))
    packed = pack_lat(place, in_l)
    pieces = gather_head(packed, heads)
    in_k = swap(after(out_k, packed), "seq")
    packed_k = pack_key(place, in_k)
    p_r, factors, v_r, partial = rest_stage(
        query, src, pieces, bias_rem, own, packed_k, heads
    )
    parts = swap(partial, "head")
    context = contexts(after(factors, partial), own[0], p_r, own[2], v_r)
    share = index_query.shape[0]
    loss, grad = index(
        h1, index_query, index_weight, own_key, after(parts, context),
        bias_own.reshape(heads, share, OWN), bias_rem,
    )
    return context, loss.reshape(-1), grad


def solution(mesh):
    placed = (
        P("seq", "head"),
        P("seq", None),
        P("seq", None),
        P(("seq", "head"), None),
        P(("seq", "head"), None),
        P("seq", None),
        P("seq"),
        P("seq"),
    )
    return jax.shard_map(
        body,
        mesh=mesh,
        in_specs=placed,
        out_specs=(P("seq", "head"), P(("seq", "head")), P(("seq", "head"), None)),
        check_vma=False,
    )
```
